256 devices in a mesh: fsdp: 64 (over y, z_lo, x, core), ctx: 4 (over z_hi).
Axes of the slice: x: 4, y: 4, z: 8 (z_hi: 4, z_lo: 2; z = z_hi * 2 + z_lo), core: 2. Of those that a mesh axis runs over, the one named last changes fastest.
Arguments:
- q_feat: bfloat16 [64, 512, 4096], P('fsdp', 'ctx'), may hold values from -6 to 6
- k_feat: bfloat16 [64, 512, 4096], P('fsdp', 'ctx'), may hold values from -6 to 6
- v_feat: bfloat16 [64, 512, 4096], P('fsdp', 'ctx'), may hold values from -6 to 6
- residue: float32 [4096, 16], P('ctx'), may hold values from -0.125 to 0.125
- rate: float32 [4096, 16], P('ctx'), may hold values from 0.00048828125 to 0.04
- w_out: bfloat16 [4096, 4096], P('fsdp', 'ctx'), may hold values from -0.09375 to 0.09375
- cotangent: bfloat16 [64, 512, 4096], P('fsdp', 'ctx')
Outputs:
- grad_q: bfloat16 [64, 512, 4096], P('fsdp', 'ctx')
- grad_k: bfloat16 [64, 512, 4096], P('fsdp', 'ctx')
- grad_v: bfloat16 [64, 512, 4096], P('fsdp', 'ctx')
- grad_weight: float32 [4096, 4096], P('fsdp', 'ctx')
- grad_residue: float32 [4096, 16], P('ctx')
- grad_rate: float32 [4096, 16], P('ctx')
The draws below stay inside these ranges and needn't reach their ends.
All inputs are finite; a program needn't handle non-finite values.
Results may differ from the reference program's by a relative error of at most 0.008.
Values may be sent and summed in bfloat16 or wider, within the bound.
A program may use at most 128 MiB of HBM per device.

```python
import math
import jax
import jax.numpy as jnp
from jax import lax

D = 4096
C = 4096
MODES = 16
TOK_DEV = 128
LENGTH = 512
SEQS = 64
N_CTX = 4


def draw_cotangent(key, part):
    key = jax.random.fold_in(key, 7)
    key_base, key_pair = jax.random.split(key, 2)
    base_draw = jax.random.truncated_normal(key_base, -6.0, 6.0, (SEQS, LENGTH, D), jnp.float32)
    top_ratio = 3.0
    rise_scale = top_ratio ** (jnp.arange(SEQS, dtype=jnp.float32) / max(SEQS - 1, 1))
    pairing = jax.random.permutation(key_pair, SEQS)
    block_index = jnp.arange(D) // (D // SEQS)
    spike_scale = jnp.where(block_index[None, :] == pairing[:, None], 3.0, 1.0)
    return (base_draw * rise_scale[:, None, None] * spike_scale[:, None, :]).astype(jnp.bfloat16)


def block_scale(own_key, dims, pieces, smallest, high):
    def one(axis_at, blocks):
        steps = jax.random.uniform(jax.random.fold_in(jax.random.fold_in(own_key, 6), axis_at), (blocks,), jnp.float32, smallest / len(pieces), high / len(pieces))
        return jnp.repeat(jnp.exp(steps), dims[axis_at] // blocks).reshape((-1,) + (1,) * (len(dims) - axis_at - 1))

    level = one(*pieces[0])
    for cut in pieces[1:]:
        level = level * one(*cut)
    return level


def normal_values(rng, extent, scale, most, cuts=(), held_as=jnp.bfloat16):
    drawn = scale * jax.random.normal(rng, extent, jnp.float32)
    if cuts:
        drawn = drawn * block_scale(rng, extent, cuts, -0.22, 0.18)
    return jnp.clip(drawn, -most, most).astype(held_as)


def setup_inputs(seed: int = 0) -> dict:
    key_of = jax.random.split(jax.random.key(seed), 8)
    return {
        "q_feat": normal_values(key_of[0], (SEQS, LENGTH, C), 1.0, 6.0, ((0, 64), (1, 4))),
        "k_feat": normal_values(key_of[1], (SEQS, LENGTH, C), 1.0, 6.0, ((0, 64), (1, 4))),
        "v_feat": normal_values(key_of[2], (SEQS, LENGTH, C), 1.0, 6.0, ((0, 64), (1, 4))),
        "residue": normal_values(key_of[3], (C, MODES), (MODES * TOK_DEV * N_CTX // 4) ** -0.5, 0.125, ((0, 4),), jnp.float32),
        "rate": jnp.clip(jnp.exp(math.log(0.04) - 4.405743 * jax.random.uniform(key_of[4], (C, MODES), jnp.float32) ** block_scale(key_of[4], (C, MODES), ((0, 4),), -0.2, 0.2)), 0.00048828125, 0.04),
        "w_out": normal_values(key_of[5], (D, C), C ** -0.5, 0.09375, ((0, 64), (1, 4))),
        "cotangent": draw_cotangent(jax.random.fold_in(key_of[7], 71), 0),
    }


def dft_tables(length):
    indices = jnp.arange(length, dtype=jnp.int32)
    product_mod = (indices[:, None] * indices[None, :]) % (2 * length)
    angles = jnp.pi * product_mod.astype(jnp.float32) / length
    cosine = jnp.cos(angles).astype(jnp.bfloat16)
    sine_table = jnp.sin(angles).astype(jnp.bfloat16)
    parity = jnp.where(indices % 2 == 0, 1.0, -1.0).astype(jnp.float32)
    return cosine, sine_table, parity


def filter_spectrum(residue, rate, length):
    indices = jnp.arange(length + 1, dtype=jnp.int32)
    angle_step = jnp.pi * indices.astype(jnp.float32) / length
    parity = jnp.where(indices % 2 == 0, 1.0, -1.0).astype(jnp.float32)[:, None, None]
    retained = jnp.exp(-rate)[None]
    margin = -jnp.expm1(-rate)[None]
    ending = jnp.exp(-rate * length)[None]
    half_sin = jnp.sin(0.5 * angle_step)[:, None, None]
    across = margin + 2.0 * retained * half_sin * half_sin
    upward = retained * jnp.sin(angle_step)[:, None, None]
    weights = residue[None] * (1.0 - ending * parity) / (across * across + upward * upward)
    real_part = jnp.sum(weights * across, axis=2)
    imag_part = -jnp.sum(weights * upward, axis=2)
    return real_part[:length], imag_part[:length], real_part[length]


def to_spectrum(cosine, sine_table, parity, signal):
    row_count = signal.shape[0]
    stacked = jnp.concatenate([cosine, sine_table], axis=0)
    product = jnp.dot(stacked, signal, preferred_element_type=jnp.float32)
    nyquist = jnp.dot(parity.astype(jnp.bfloat16)[None, :], signal, preferred_element_type=jnp.float32)[0]
    return product[:row_count], -product[row_count:], nyquist


def from_spectrum(cosine, sine_table, parity, real_part, imag_part, nyquist):
    row_count = real_part.shape[0]
    doubling = jnp.where(jnp.arange(row_count) == 0, 1.0, 2.0).astype(jnp.float32)[:, None]
    packed = jnp.concatenate([real_part * doubling, -(imag_part * doubling)], axis=0).astype(jnp.bfloat16)
    wide_table = jnp.concatenate([cosine, sine_table], axis=1)
    summed = jnp.dot(wide_table, packed, preferred_element_type=jnp.float32)
    return (summed + parity[:, None] * nyquist[None, :]) / (2.0 * row_count)


def reference(q_feat, k_feat, v_feat, residue, rate, w_out, cotangent):
    length = q_feat.shape[1]
    cosine, sine_table, parity = dft_tables(length)
    filt_real, filt_imag, filt_nyq = filter_spectrum(residue, rate, length)
    positions = jnp.arange(length).astype(jnp.float32)[:, None, None]
    decay_table = jnp.exp(-rate[None] * positions)

    def per_sequence(running, inputs):
        grad_total, resid_total, rate_total = running
        query_seq, keys_seq, values_seq, cot_seq = inputs
        mixed = (keys_seq.astype(jnp.float32) * values_seq.astype(jnp.float32)).astype(jnp.bfloat16)
        mix_real, mix_imag, mix_nyq = to_spectrum(cosine, sine_table, parity, mixed)
        conv_out = from_spectrum(cosine, sine_table, parity,
                                 mix_real * filt_real - mix_imag * filt_imag,
                                 mix_real * filt_imag + mix_imag * filt_real,
                                 mix_nyq * filt_nyq)
        gated_out = (query_seq.astype(jnp.float32) * conv_out).astype(jnp.bfloat16)
        grad_gated = jnp.dot(cot_seq, w_out, preferred_element_type=jnp.float32)
        grad_total = grad_total + jnp.dot(cot_seq.T, gated_out, preferred_element_type=jnp.float32)
        grad_query = (grad_gated * conv_out).astype(jnp.bfloat16)
        grad_conv = (grad_gated * query_seq.astype(jnp.float32)).astype(jnp.bfloat16)
        spec_real, spec_imag, spec_nyq = to_spectrum(cosine, sine_table, parity, grad_conv)
        grad_mix = from_spectrum(cosine, sine_table, parity,
                                 filt_real * spec_real + filt_imag * spec_imag,
                                 filt_real * spec_imag - filt_imag * spec_real,
                                 filt_nyq * spec_nyq).astype(jnp.bfloat16)
        grad_kernel = from_spectrum(cosine, sine_table, parity,
                                    mix_real * spec_real + mix_imag * spec_imag,
                                    mix_real * spec_imag - mix_imag * spec_real,
                                    mix_nyq * spec_nyq)
        weighted = grad_kernel[:, :, None] * decay_table
        resid_total = resid_total + jnp.sum(weighted, axis=0)
        rate_total = rate_total + jnp.sum(weighted * positions, axis=0)
        grad_keys = (grad_mix.astype(jnp.float32) * values_seq.astype(jnp.float32)).astype(jnp.bfloat16)
        grad_values = (grad_mix.astype(jnp.float32) * keys_seq.astype(jnp.float32)).astype(jnp.bfloat16)
        return (grad_total, resid_total, rate_total), (grad_query, grad_keys, grad_values)

    start_state = (jnp.zeros(w_out.shape, jnp.float32), jnp.zeros(residue.shape, jnp.float32),
                   jnp.zeros(residue.shape, jnp.float32))
    finals, grads = lax.scan(per_sequence, start_state, (q_feat, k_feat, v_feat, cotangent))
    grad_weight, grad_residue, rate_sum = finals
    grad_q, grad_k, grad_v = grads
    grad_rate = -residue * rate_sum
    return grad_q, grad_k, grad_v, grad_weight, grad_residue, grad_rate
```

```python
import jax
import jax.numpy as jnp
from jax import lax
from jax.experimental import pallas as pl
from jax.experimental.pallas import tpu as pltpu
from jax.sharding import PartitionSpec as P

MESH = pl.DeviceIdType.MESH
F32, BF16 = jnp.float32, jnp.bfloat16
TOK = 128
WIDTH = 4096
TILES = 32
MODES = 16
COLS = 512
N_SEND = 96
N_RECV = 112


class Links:
    def __init__(self, send_sems, recv_sems):
        self.send_sems, self.recv_sems = send_sems, recv_sems
        self.sent, self.n_send, self.n_recv = [], 0, 0

    def slot(self, count=1):
        first = self.n_recv
        self.n_recv += count
        assert self.n_recv <= N_RECV
        return first

    def send(self, src, dst, recv, to, only=None):
        sem = self.send_sems.at[self.n_send]
        self.n_send += 1
        assert self.n_send <= N_SEND
        copy = pltpu.make_async_remote_copy(
            src_ref=src, dst_ref=dst, send_sem=sem, recv_sem=self.recv_sems.at[recv],
            device_id=to, device_id_type=MESH)
        if only is None:
            copy.start()
        else:
            pl.when(only)(copy.start)
        self.sent.append((copy, only))

    def local(self, src, dst, recv, only=None):
        copy = pltpu.make_async_copy(src, dst, self.recv_sems.at[recv])
        if only is None:
            copy.start()
        else:
            pl.when(only)(copy.start)

    def wait(self, dst, recv):
        pltpu.make_async_copy(dst, dst, self.recv_sems.at[recv]).wait()

    def finish(self):
        for copy, only in self.sent:
            if only is None:
                copy.wait_send()
            else:
                pl.when(only)(copy.wait_send)


def kernel(q_hbm, k_hbm, v_hbm, par_hbm, w_hbm, cot_hbm,
           gq_hbm, gk_hbm, gv_hbm, gw_hbm, ab_hbm,
           qb, kb, vb, par, cotb, wbuf, xs, cs, gs, es, er, es2, er2, carry, yend,
           gat_send, gat, gsend, grecv, gwp, ra, rb, from_lo, from_hi, vsum,
           zsend, zrecv, fin, gwo, ab, tp_recv, r1, ctx_recv, r2, g_recv, r3, tot,
           gq, gk, gv, send_sems, recv_sems):
    f, zh = lax.axis_index("fsdp"), lax.axis_index("ctx")
    y, zl, x, core = f // 16, (f // 8) % 2, (f // 2) % 4, f % 2
    b, g = f % 8, f // 8
    z = zh * 2 + zl
    links = Links(send_sems, recv_sems)

    def group(delta):
        return (g * 8 + (b + delta) % 8, zh)

    def outer(delta):
        return (((g + delta) % 8) * 8 + b, zh)

    def along_z(delta):
        to = (z + delta) % 8
        return (y * 16 + (to % 2) * 8 + b, to // 2)

    def along_y(delta):
        return (((y + delta) % 4) * 16 + zl * 8 + b, zh)

    def along_x(delta):
        return (g * 8 + ((x + delta) % 4) * 2 + core, zh)

    sibling = (g * 8 + x * 2 + 1 - core, zh)

    def crossed(h):
        return (g * 8 + zh * 2 + h, x)

    barrier = pltpu.get_barrier_semaphore()
    peers = [group(delta) for delta in range(1, 8)] + [along_z(delta) for delta in range(1, 8)]
    for delta in range(1, 4):
        for level in range(2):
            peers.append((((y + delta) % 4) * 16 + level * 8 + b, zh))
    for to in peers:
        pl.semaphore_signal(barrier, inc=1, device_id=to, device_id_type=MESH)

    @pl.when(x != zh)
    def _():
        for h in range(2):
            pl.semaphore_signal(barrier, inc=1, device_id=crossed(h), device_id_type=MESH)
        pl.semaphore_wait(barrier, len(peers) + 2)

    @pl.when(x == zh)
    def _():
        pl.semaphore_wait(barrier, len(peers))

    par_at = links.slot(4)
    for delta in range(1, 4):
        links.send(par_hbm, par.at[zh], par_at + delta, (f, (zh + delta) % 4))
    links.local(par_hbm, par.at[zh], par_at)

    w_at = links.slot(2)
    w_rows = pl.ds(pl.multiple_of(f * 64, 64), 64)
    for h in range(2):
        here = jnp.logical_and(x == zh, core == h)
        src = w_hbm.at[:, pl.ds(h * COLS, COLS)]
        links.send(src, wbuf.at[w_rows, :], w_at + core, crossed(h), only=jnp.logical_not(here))
        links.local(src, wbuf.at[w_rows, :], w_at + core, only=here)

    half = TOK // 2
    x_at = links.slot(4)
    own = cotb.at[b]

    def rows_of(ref, h):
        return ref.at[pl.ds(h * half, half), :]

    for to, h, at in ((1, 0, 0), (-1, 1, 3), (1, 1, 1), (-1, 0, 2)):
        links.send(rows_of(cot_hbm, h), rows_of(own, h), x_at + at, along_x(to))
    cot_at = links.slot(1)
    links.local(cot_hbm, own, cot_at)
    sib_at = links.slot(7)
    links.send(cot_hbm, own, sib_at, sibling)
    load_at = links.slot(3)
    for i, (src, dst) in enumerate(((k_hbm, kb), (v_hbm, vb), (q_hbm, qb))):
        links.local(src, dst, load_at + i)

    links.wait(kb, load_at)
    links.wait(vb, load_at + 1)

    def put(ref, t0, tile, value):
        for i in range(2):
            start = (t0 + 8 * i) * TILES + tile
            ref[pl.ds(start, 8, stride=TILES), :] = value[8 * i:8 * i + 8]

    def get(ref, t0, tile):
        parts = [ref[pl.ds((t0 + 8 * i) * TILES + tile, 8, stride=TILES), :] for i in range(2)]
        return jnp.concatenate(parts, axis=0)

    def each_stripe(body):
        def step(i, _):
            t0 = pl.multiple_of(i * 16, 16)
            for tile in range(TILES):
                body(t0, tile, pl.ds(t0, 16), pl.ds(tile * 128, 128))
            return 0
        lax.fori_loop(0, TOK // 16, step, 0)

    def mix(t0, tile, rows, lanes):
        product = kb[rows, lanes].astype(F32) * vb[rows, lanes].astype(F32)
        put(xs, t0, tile, product.astype(BF16).astype(F32))

    each_stripe(mix)

    for delta in range(1, 4):
        links.wait(par.at[(zh + 4 - delta) % 4], par_at + delta)
    links.wait(par.at[zh], par_at)

    def row_at(t, block):
        return pl.ds(pl.multiple_of(t * TILES + block * 8, 8), 8)

    def each_block(body):
        def step(block, _):
            body(block)
            return 0
        lax.fori_loop(0, 4, step, 0)

    def run_states(src, backward, es):
        def one(block):
            decay = jnp.exp(-par[block, 0:MODES])

            def step(i, state):
                for r in range(8):
                    t = i * 8 + r
                    t = TOK - 1 - t if backward else t
                    state = state * decay + src[row_at(t, block), :][None]
                return state

            state = lax.fori_loop(0, TOK // 8, step, jnp.zeros((MODES, 8, 128), F32))
            es[pl.ds(pl.multiple_of(block * 128, 128), 128), :] = state.reshape(128, 128).astype(BF16)
        each_block(one)

    def exchange_states(sign, es, er):
        at = links.slot(3)
        for delta in range(1, 4):
            to = zh + sign * delta
            ok = to < 4 if sign > 0 else to >= 0
            links.send(es, er.at[delta - 1], at + delta - 1, (f, (to + 4) % 4), only=ok)
        return at

    def gather_states(sign, at, er):
        carry[...] = jnp.zeros(carry.shape, F32)
        for delta in range(1, 4):
            source = zh - sign * delta

            @pl.when(source >= 0 if sign > 0 else source < 4)
            def _():
                links.wait(er.at[delta - 1], at + delta - 1)

                def one(block):
                    rows = pl.ds(pl.multiple_of(block * 128, 128), 128)
                    term = er[delta - 1, rows, :].astype(F32).reshape(MODES, 8, 128)
                    if delta > 1:
                        term = term * jnp.exp(par[block, 0:MODES] * (-float(TOK) * (delta - 1)))
                    carry[block] += term
                each_block(one)

    run_states(xs, False, es)
    s_at = exchange_states(1, es, er)

    links.wait(wbuf.at[pl.ds(0, 64), :], w_at)
    links.wait(wbuf.at[pl.ds(0, 64), :], w_at + 1)

    def slab(zz):
        return pl.ds(pl.multiple_of(y * 1024 + (zz % 2) * 512 + (zz // 2) * 128, 128), 128)

    wz_at = links.slot(7)
    for delta in (1, 7, 2, 6, 3, 5, 4):
        links.send(wbuf.at[slab(z), :], wbuf.at[slab(z), :], wz_at + delta - 1, along_z(delta))

    gather_states(1, s_at, er)

    def tree(v):
        while v.shape[0] > 1:
            n = v.shape[0] // 2
            v = v[:n] + v[n:]
        return v[0]

    def convolve(block):
        decay = jnp.exp(-par[block, 0:MODES])
        weight = par[block, MODES:2 * MODES]

        def step(i, state):
            for r in range(8):
                rows = row_at(i * 8 + r, block)
                state = state * decay + xs[rows, :][None]
                cs[rows, :] = tree(state * weight)
            return state

        yend[block] = lax.fori_loop(0, TOK // 8, step, carry[block])

    each_block(convolve)

    links.wait(qb, load_at + 2)

    def gate(t0, tile, rows, lanes):
        gated = qb[rows, lanes].astype(F32) * get(cs, t0, tile)
        gat_send[tile // 4, rows, pl.ds((tile % 4) * 128, 128)] = gated.astype(BF16)

    each_stripe(gate)

    gat_at = links.slot(8)
    links.local(gat_send.at[b], gat.at[b], gat_at)
    for delta in range(1, 8):
        links.send(gat_send.at[(b + delta) % 8], gat.at[b], gat_at + delta, group(delta))

    left, right, far = ((x + 3) % 4) * 2 + core, ((x + 1) % 4) * 2 + core, ((x + 2) % 4) * 2 + core
    far_at = links.slot(2)
    links.wait(rows_of(cotb.at[left], 0), x_at)
    links.send(rows_of(cotb.at[left], 0), rows_of(cotb.at[left], 0), far_at, along_x(1))
    links.send(rows_of(cotb.at[left], 0), rows_of(cotb.at[left], 0), sib_at + 1, sibling)
    links.wait(rows_of(cotb.at[right], 1), x_at + 3)
    links.send(rows_of(cotb.at[right], 1), rows_of(cotb.at[right], 1), far_at + 1, along_x(-1))
    links.send(rows_of(cotb.at[right], 1), rows_of(cotb.at[right], 1), sib_at + 2, sibling)
    links.wait(rows_of(cotb.at[left], 1), x_at + 1)
    links.send(rows_of(cotb.at[left], 1), rows_of(cotb.at[left], 1), sib_at + 3, sibling)
    links.wait(rows_of(cotb.at[right], 0), x_at + 2)
    links.send(rows_of(cotb.at[right], 0), rows_of(cotb.at[right], 0), sib_at + 4, sibling)

    for delta in range(1, 8):
        links.wait(wbuf.at[slab((z + 8 - delta) % 8), :], wz_at + delta - 1)

    def w_half(yy, h):
        return wbuf.at[pl.ds(pl.multiple_of(((yy + 4) % 4) * 1024 + h * 512, 512), 512), :]

    wy_at = links.slot(4)
    for to, h, at in ((1, 0, 0), (-1, 1, 3), (1, 1, 1), (-1, 0, 2)):
        links.send(w_half(y, h), w_half(y, h), wy_at + at, along_y(to))

    for h in range(2):
        links.wait(rows_of(cotb.at[far], h), far_at + h)
        links.send(rows_of(cotb.at[far], h), rows_of(cotb.at[far], h), sib_at + 5 + h, sibling)

    wf_at = links.slot(2)
    links.wait(w_half(y - 1, 0), wy_at)
    links.send(w_half(y - 1, 0), w_half(y - 1, 0), wf_at, along_y(1))
    links.wait(w_half(y + 1, 1), wy_at + 3)
    links.send(w_half(y + 1, 1), w_half(y + 1, 1), wf_at + 1, along_y(-1))

    links.wait(own, cot_at)
    other = 1 - 2 * core
    links.wait(cotb.at[b + other], sib_at)
    links.wait(rows_of(cotb.at[left + other], 0), sib_at + 1)
    links.wait(rows_of(cotb.at[right + other], 1), sib_at + 2)
    links.wait(rows_of(cotb.at[left + other], 1), sib_at + 3)
    links.wait(rows_of(cotb.at[right + other], 0), sib_at + 4)
    for h in range(2):
        links.wait(rows_of(cotb.at[far + other], h), sib_at + 5 + h)
    for delta in range(8):
        links.wait(gat.at[(b + 8 - delta) % 8], gat_at + delta)

    def part_rows(delta):
        return pl.multiple_of(((y + delta + 4) % 4) * 1024, 1024)

    def weight_part(delta, dst, base):
        def step(i, _):
            at = pl.multiple_of(part_rows(delta) + i * 256, 256)
            lhs = cotb[:, :, pl.ds(at, 256)].reshape(8 * TOK, 256)
            out = lax.dot_general(lhs, gat[...].reshape(8 * TOK, COLS), (((0,), (0,)), ((), ())),
                                  preferred_element_type=F32)
            dst[pl.ds(pl.multiple_of(base + i * 256, 256), 256), :] = out.astype(dst.dtype)
            return 0
        lax.fori_loop(0, 4, step, 0)

    def part_half(delta, h):
        return gwp.at[pl.ds(pl.multiple_of(part_rows(delta) + h * 512, 512), 512), :]

    def half_of(ref, h):
        return ref.at[pl.ds(h * 512, 512), :]

    gy_at = links.slot(6)
    weight_part(2, gwp, part_rows(2))
    links.send(part_half(2, 0), ra, gy_at, along_y(1))
    links.send(part_half(2, 1), rb, gy_at + 1, along_y(-1))
    weight_part(1, gwp, part_rows(1))
    links.send(part_half(1, 1), half_of(from_lo, 1), gy_at + 2, along_y(1))
    weight_part(-1, gwp, part_rows(-1))
    links.send(part_half(-1, 0), half_of(from_hi, 0), gy_at + 3, along_y(-1))
    weight_part(0, vsum, 0)

    links.wait(w_half(y - 1, 1), wy_at + 1)
    links.wait(w_half(y + 1, 0), wy_at + 2)
    links.wait(w_half(y + 2, 0), wf_at)
    links.wait(w_half(y + 2, 1), wf_at + 1)

    def project(i, _):
        total = jnp.zeros((2 * TOK, COLS), F32)
        for part in range(4):
            lhs = cotb[pl.ds(i * 2, 2), :, pl.ds(part * 1024, 1024)].reshape(2 * TOK, 1024)
            total += jnp.dot(lhs, wbuf[pl.ds(part * 1024, 1024), :], preferred_element_type=F32)
        gsend[pl.ds(i * 2, 2)] = total.astype(BF16).reshape(2, TOK, COLS)
        return 0

    lax.fori_loop(0, 4, project, 0)
    g_at = links.slot(8)
    links.local(gsend.at[b], grecv.at[b], g_at)
    for delta in range(1, 8):
        links.send(gsend.at[(b + delta) % 8], grecv.at[b], g_at + delta, group(delta))

    def add_half(delta, h, term):
        def step(i, _):
            rows = pl.ds(pl.multiple_of(part_rows(delta) + h * 512 + i * 64, 64), 64)
            theirs = term[pl.ds(pl.multiple_of(i * 64, 64), 64), :].astype(F32)
            gwp[rows, :] = (gwp[rows, :].astype(F32) + theirs).astype(BF16)
            return 0
        lax.fori_loop(0, 8, step, 0)

    links.wait(ra, gy_at)
    add_half(1, 0, ra)
    links.send(part_half(1, 0), half_of(from_lo, 0), gy_at + 4, along_y(1))
    links.wait(rb, gy_at + 1)
    add_half(-1, 1, rb)
    links.send(part_half(-1, 1), half_of(from_hi, 1), gy_at + 5, along_y(-1))

    for delta in range(8):
        links.wait(grecv.at[(b + 8 - delta) % 8], g_at + delta)

    def grad_gate(t0, tile, rows, lanes):
        grad = grecv[tile // 4, rows, pl.ds((tile % 4) * 128, 128)].astype(F32)
        gq[rows, lanes] = (grad * get(cs, t0, tile)).astype(BF16)
        put(gs, t0, tile, (grad * qb[rows, lanes].astype(F32)).astype(BF16).astype(F32))

    each_stripe(grad_gate)
    out_at = links.slot(3)
    links.local(gq, gq_hbm, out_at)

    run_states(gs, True, es2)
    t_at = exchange_states(-1, es2, er2)

    links.wait(half_of(from_lo, 1), gy_at + 2)
    links.wait(half_of(from_lo, 0), gy_at + 4)
    links.wait(half_of(from_hi, 0), gy_at + 3)
    links.wait(half_of(from_hi, 1), gy_at + 5)

    def add_y(i, _):
        rows = pl.ds(pl.multiple_of(i * 64, 64), 64)
        vsum[rows, :] += from_lo[rows, :].astype(F32) + from_hi[rows, :].astype(F32)
        return 0

    lax.fori_loop(0, 16, add_y, 0)

    def z_rows(zz):
        return pl.ds(pl.multiple_of((zz % 2) * 512 + (zz // 2) * 128, 128), 128)

    gz_at = links.slot(7)
    for delta in (4, 3, 5, 2, 6, 1, 7):
        zsend[delta - 1] = vsum[z_rows((z + delta) % 8), :].astype(BF16)
        links.send(zsend.at[delta - 1], zrecv.at[delta - 1], gz_at + delta - 1, along_z(delta))

    gather_states(-1, t_at, er2)

    part = 4

    def adjoint(block):
        for m in range(0, MODES, part):
            rate = par[block, m:m + part]
            decay, growth = jnp.exp(-rate), jnp.exp(rate)
            weight = par[block, MODES + m:MODES + m + part]

            def step(i, carried):
                p, s, da, db = carried
                for r in range(8):
                    rows = row_at(TOK - 1 - (i * 8 + r), block)
                    xt = xs[rows, :][None]
                    p = p * decay + gs[rows, :][None]
                    da = da + p * xt
                    s = (s - xt) * growth
                    db = db + p * s
                    out = tree(p * weight)
                    if m:
                        out = out + cs[rows, :]
                    cs[rows, :] = out
                return p, s, da, db

            zero = jnp.zeros((part, 8, 128), F32)
            start = (carry[block, m:m + part], yend[block, m:m + part], zero, zero)
            _, _, da, db = lax.fori_loop(0, TOK // 8, step, start)
            ab[block, m:m + part] = da
            ab[block, MODES + m:MODES + m + part] = db * decay

    each_block(adjoint)

    tp_at = links.slot(7)
    for delta in range(1, 8):
        to = pl.ds(((b + delta) % 8) * 4, 4)
        links.send(ab.at[:, to], tp_recv.at[delta - 1], tp_at + delta - 1, group(delta))

    def grads(t0, tile, rows, lanes):
        grad = get(cs, t0, tile).astype(BF16).astype(F32)
        gk[rows, lanes] = (grad * vb[rows, lanes].astype(F32)).astype(BF16)
        gv[rows, lanes] = (grad * kb[rows, lanes].astype(F32)).astype(BF16)

    each_stripe(grads)
    links.local(gk, gk_hbm, out_at + 1)
    links.local(gv, gv_hbm, out_at + 2)

    r1[...] = ab[:, pl.ds(b * 4, 4)]
    for delta in range(1, 8):
        links.wait(tp_recv.at[delta - 1], tp_at + delta - 1)
        r1[...] += tp_recv[delta - 1]
    c_at = links.slot(3)
    for delta in range(1, 4):
        links.send(r1.at[(zh + delta) % 4], ctx_recv.at[delta - 1], c_at + delta - 1, (f, (zh + delta) % 4))

    fin[...] = vsum[z_rows(z), :]
    for delta in range(1, 8):
        links.wait(zrecv.at[delta - 1], gz_at + delta - 1)
        fin[...] += zrecv[delta - 1].astype(F32)
    fin_at = links.slot(2)
    for h in range(2):
        here = jnp.logical_and(x == zh, core == h)
        src = fin.at[pl.ds(h * 64, 64), :]
        links.send(src, gwo.at[core], fin_at + core, crossed(h), only=jnp.logical_not(here))
        links.local(src, gwo.at[core], fin_at + core, only=here)

    r2[...] = r1[zh]
    for delta in range(1, 4):
        links.wait(ctx_recv.at[delta - 1], c_at + delta - 1)
        r2[...] += ctx_recv[delta - 1]
    o_at = links.slot(7)
    for delta in range(1, 8):
        links.send(r2, g_recv.at[delta - 1], o_at + delta - 1, outer(delta))

    gwo_at = links.slot(2)
    for h in range(2):
        links.wait(gwo.at[h], fin_at + h)
        links.local(gwo.at[h], gw_hbm.at[:, pl.ds(h * COLS, COLS)], gwo_at + h)

    for delta in range(1, 8):
        links.wait(g_recv.at[delta - 1], o_at + delta - 1)
    total = jnp.zeros((4, 8, 128), F32)
    for source in range(8):
        delta = (g + 8 - source) % 8
        theirs = g_recv[jnp.maximum(delta - 1, 0)]
        total = total + jnp.where(delta == 0, r2[...], theirs)
    r3[...] = total
    e_at = links.slot(8)
    for delta in range(1, 8):
        links.send(r3, tot.at[pl.ds(b * 4, 4)], e_at + delta, group(delta))
    links.local(r3, tot.at[pl.ds(b * 4, 4)], e_at)
    for delta in range(8):
        links.wait(tot.at[pl.ds(((b + 8 - delta) % 8) * 4, 4)], e_at + delta)
    ab_at = links.slot(1)
    links.local(tot, ab_hbm, ab_at)

    links.wait(gq, out_at)
    links.wait(gk, out_at + 1)
    links.wait(gv, out_at + 2)
    for h in range(2):
        links.wait(gwo.at[h], gwo_at + h)
    links.wait(tot, ab_at)
    links.finish()


def shards(q_feat, k_feat, v_feat, residue, rate, w_out, cotangent):
    params = jnp.concatenate([rate.T, residue.T], axis=0).reshape(2 * MODES, 8, 128)
    anyspace = pl.BlockSpec(memory_space=pl.ANY)
    flat = (TOK, WIDTH)
    act = jax.ShapeDtypeStruct(flat, BF16)
    v = pltpu.VMEM
    grad_q, grad_k, grad_v, grad_weight, sums = pl.pallas_call(
        kernel,
        out_shape=(act, act, act, jax.ShapeDtypeStruct((64, 1024), F32),
                   jax.ShapeDtypeStruct((2 * MODES, 8, 128), F32)),
        in_specs=[anyspace] * 6,
        out_specs=[anyspace] * 5,
        scratch_shapes=[
            v(flat, BF16), v(flat, BF16), v(flat, BF16),
            v((4, 2 * MODES, 8, 128), F32),
            v((8, TOK, WIDTH), BF16), v((WIDTH, COLS), BF16),
            v((WIDTH, 128), F32), v((WIDTH, 128), F32), v((WIDTH, 128), F32),
            v((512, 128), BF16), v((3, 512, 128), BF16),
            v((512, 128), BF16), v((3, 512, 128), BF16),
            v((4, MODES, 8, 128), F32), v((4, MODES, 8, 128), F32),
            v((8, TOK, COLS), BF16), v((8, TOK, COLS), BF16),
            v((8, TOK, COLS), BF16), v((8, TOK, COLS), BF16),
            v((WIDTH, COLS), BF16),
            v((512, COLS), BF16), v((512, COLS), BF16),
            v((1024, COLS), BF16), v((1024, COLS), BF16),
            v((1024, COLS), F32),
            v((7, 128, COLS), BF16), v((7, 128, COLS), BF16),
            v((128, COLS), F32), v((2, 64, COLS), F32),
            v((4, 2 * MODES, 8, 128), F32),
            v((7, 4, 4, 8, 128), F32), v((4, 4, 8, 128), F32),
            v((3, 4, 8, 128), F32), v((4, 8, 128), F32),
            v((7, 4, 8, 128), F32), v((4, 8, 128), F32),
            v((2 * MODES, 8, 128), F32),
            v(flat, BF16), v(flat, BF16), v(flat, BF16),
            pltpu.SemaphoreType.DMA((N_SEND,)),
            pltpu.SemaphoreType.DMA((N_RECV,)),
        ],
        compiler_params=pltpu.CompilerParams(
            collective_id=0, has_side_effects=True, vmem_limit_bytes=60 * 1024 * 1024),
    )(q_feat[0], k_feat[0], v_feat[0], params, w_out, cotangent[0])
    sums = sums.reshape(2, MODES, 1024)
    grad_residue = sums[0].T
    grad_rate = -residue * sums[1].T
    return grad_q[None], grad_k[None], grad_v[None], grad_weight, grad_residue, grad_rate


def solution(mesh):
    act, modes, proj = P("fsdp", "ctx", None), P("ctx", None), P("fsdp", "ctx")
    return jax.shard_map(
        shards,
        mesh=mesh,
        in_specs=(act, act, act, modes, modes, proj, act),
        out_specs=(act, act, act, proj, modes, modes),
        check_vma=False,
    )
```

```python
import jax
import jax.numpy as jnp
from jax import lax
from jax.experimental import pallas as pl
from jax.experimental.pallas import tpu as pltpu
from jax.sharding import PartitionSpec as P

MESH = pl.DeviceIdType.MESH
F32, BF16 = jnp.float32, jnp.bfloat16
TOK = 128
WIDTH = 4096
TILES = 32
MODES = 16
COLS = 512
N_SEND = 256
N_RECV = 256


class Links:
    def __init__(self, send_sems, recv_sems):
        self.send_sems, self.recv_sems = send_sems, recv_sems
        self.sent, self.n_send, self.n_recv = [], 0, 0

    def slot(self, count=1):
        first = self.n_recv
        self.n_recv += count
        assert self.n_recv <= N_RECV
        return first

    def send(self, src, dst, recv, to, only=None):
        sem = self.send_sems.at[self.n_send]
        self.n_send += 1
        assert self.n_send <= N_SEND
        copy = pltpu.make_async_remote_copy(
            src_ref=src, dst_ref=dst, send_sem=sem, recv_sem=self.recv_sems.at[recv],
            device_id=to, device_id_type=MESH)
        if only is None:
            copy.start()
        else:
            pl.when(only)(copy.start)
        self.sent.append((copy, only))

    def local(self, src, dst, recv, only=None):
        copy = pltpu.make_async_copy(src, dst, self.recv_sems.at[recv])
        if only is None:
            copy.start()
        else:
            pl.when(only)(copy.start)

    def wait(self, dst, recv):
        pltpu.make_async_copy(dst, dst, self.recv_sems.at[recv]).wait()

    def finish(self):
        for copy, only in self.sent:
            if only is None:
                copy.wait_send()
            else:
                pl.when(only)(copy.wait_send)


def kernel(q_hbm, k_hbm, v_hbm, par_hbm, w_hbm, cot_hbm,
           gq_hbm, gk_hbm, gv_hbm, gw_hbm, ab_hbm,
           qb, kb, vb, par, cotb, wbuf, xs, cs, gs, es, er, es2, er2, carry, yend,
           gat_send, gat, gsend, grecv, gwp, ra, rb, from_lo, from_hi, vsum,
           zsend, zrecv, fin, gwo, ab, tp_recv, r1, ctx_recv, r2, g_recv, r3, tot,
           gq, gk, gv, send_sems, recv_sems):
    f, zh = lax.axis_index("fsdp"), lax.axis_index("ctx")
    y, zl, x, core = f // 16, (f // 8) % 2, (f // 2) % 4, f % 2
    b, g = f % 8, f // 8
    z = zh * 2 + zl
    links = Links(send_sems, recv_sems)

    def group(delta):
        return (g * 8 + (b + delta) % 8, zh)

    def outer(delta):
        return (((g + delta) % 8) * 8 + b, zh)

    def along_z(delta):
        to = (z + delta) % 8
        return (y * 16 + (to % 2) * 8 + b, to // 2)

    def along_y(delta):
        return (((y + delta) % 4) * 16 + zl * 8 + b, zh)

    def along_x(delta):
        return (g * 8 + ((x + delta) % 4) * 2 + core, zh)

    sibling = (g * 8 + x * 2 + 1 - core, zh)

    def crossed(h):
        return (g * 8 + zh * 2 + h, x)

    barrier = pltpu.get_barrier_semaphore()
    peers = [group(delta) for delta in range(1, 8)] + [along_z(delta) for delta in range(1, 8)]
    for delta in range(1, 4):
        for level in range(2):
            peers.append((((y + delta) % 4) * 16 + level * 8 + b, zh))
    for to in peers:
        pl.semaphore_signal(barrier, inc=1, device_id=to, device_id_type=MESH)

    @pl.when(x != zh)
    def _():
        for h in range(2):
            pl.semaphore_signal(barrier, inc=1, device_id=crossed(h), device_id_type=MESH)

    load_at = links.slot(3)
    for i, (src, dst) in enumerate(((k_hbm, kb), (v_hbm, vb), (q_hbm, qb))):
        links.local(src, dst, load_at + i)
    own = cotb.at[b]
    cot_at = links.slot(1)
    links.local(cot_hbm, own, cot_at)
    own_par_at = links.slot(1)
    links.local(par_hbm, par.at[zh], own_par_at)

    links.wait(kb, load_at)
    links.wait(vb, load_at + 1)

    def put(ref, t0, tile, value):
        for i in range(2):
            start = (t0 + 8 * i) * TILES + tile
            ref[pl.ds(start, 8, stride=TILES), :] = value[8 * i:8 * i + 8]

    def get(ref, t0, tile):
        parts = [ref[pl.ds((t0 + 8 * i) * TILES + tile, 8, stride=TILES), :] for i in range(2)]
        return jnp.concatenate(parts, axis=0)

    def each_tile(body, block):
        def step(i, _):
            t0 = pl.multiple_of(i * 16, 16)
            for k in range(8):
                lanes = pl.ds(pl.multiple_of(block * 1024 + k * 128, 128), 128)
                body(t0, block * 8 + k, k, pl.ds(t0, 16), lanes)
            return 0
        lax.fori_loop(0, TOK // 16, step, 0)

    def each_block(body):
        def step(block, _):
            body(block)
            return 0
        lax.fori_loop(0, 4, step, 0)

    def mix(t0, tile, k, rows, lanes):
        product = kb[rows, lanes].astype(F32) * vb[rows, lanes].astype(F32)
        put(xs, t0, tile, product.astype(BF16).astype(F32))

    each_block(lambda block: each_tile(mix, block))

    @pl.when(x != zh)
    def _():
        pl.semaphore_wait(barrier, len(peers) + 2)

    @pl.when(x == zh)
    def _():
        pl.semaphore_wait(barrier, len(peers))

    par_at = links.slot(3)
    sib_par_at = links.slot(3)

    def par_half(j, c):
        return par.at[j, pl.ds(c * MODES, MODES)]

    w_at = links.slot(2)
    w_rows = pl.ds(pl.multiple_of(f * 64, 64), 64)
    for h in range(2):
        here = jnp.logical_and(x == zh, core == h)
        src = w_hbm.at[:, pl.ds(h * COLS, COLS)]
        links.send(src, wbuf.at[w_rows, :], w_at + core, crossed(h), only=jnp.logical_not(here))
        links.local(src, wbuf.at[w_rows, :], w_at + core, only=here)
    for delta in range(1, 4):
        links.send(par_hbm.at[pl.ds(core * MODES, MODES)], par_half(zh, core), par_at + delta - 1,
                   (f, (zh + delta) % 4))

    half = TOK // 2
    x_at = links.slot(4)

    def rows_of(ref, h):
        return ref.at[pl.ds(h * half, half), :]

    def send_x(to, h, at):
        links.send(rows_of(cot_hbm, h), rows_of(own, h), x_at + at, along_x(to))

    send_x(1, 0, 0)
    send_x(-1, 1, 3)
    sib_at = links.slot(7)

    links.wait(wbuf.at[pl.ds(0, 64), :], w_at)
    links.wait(wbuf.at[pl.ds(0, 64), :], w_at + 1)

    def w_block(dy, dz, h=None):
        zz = (z + dz + 8) % 8
        start = ((y + dy + 4) % 4) * 1024 + (zz % 2) * 512 + (zz // 2) * 128
        if h is None:
            return wbuf.at[pl.ds(pl.multiple_of(start, 128), 128), :]
        return wbuf.at[pl.ds(pl.multiple_of(start + h * 64, 64), 64), :]

    up_at = links.slot(5)
    down_at = links.slot(5)
    wy_at = links.slot(8 * 6)

    def pass_z(step):
        for to, at in ((1, up_at), (-1, down_at)):
            ref = w_block(0, -to * step, None if step < 3 else (1 - to) // 2)
            links.send(ref, ref, at + step, along_z(to))

    def wait_z(step):
        for to, at in ((1, up_at), (-1, down_at)):
            links.wait(w_block(0, -to * step, None if step < 4 else (1 - to) // 2), at + step - 1)

    def send_y(dz):
        base = wy_at + (dz + 8) % 8 * 6
        for to, h, at in ((1, 0, 0), (-1, 1, 1), (1, 1, 2), (-1, 0, 3)):
            links.send(w_block(0, dz, h), w_block(0, dz, h), base + at, along_y(to))

    def pass_y(dz):
        base = wy_at + (dz + 8) % 8 * 6
        links.wait(w_block(-1, dz, 0), base)
        links.send(w_block(-1, dz, 0), w_block(-1, dz, 0), base + 4, along_y(1))
        links.wait(w_block(1, dz, 1), base + 1)
        links.send(w_block(1, dz, 1), w_block(1, dz, 1), base + 5, along_y(-1))

    def wait_y(dz):
        base = wy_at + (dz + 8) % 8 * 6
        links.wait(w_block(-1, dz, 1), base + 2)
        links.wait(w_block(1, dz, 0), base + 3)
        links.wait(w_block(2, dz, 0), base + 4)
        links.wait(w_block(2, dz, 1), base + 5)

    pass_z(0)
    send_y(0)
    send_x(1, 1, 1)
    send_x(-1, 0, 2)
    links.send(cot_hbm, own, sib_at, sibling)

    for delta in range(1, 4):
        source = (zh + 4 - delta) % 4
        links.wait(par_half(source, core), par_at + delta - 1)
        links.send(par_half(source, core), par_half(source, core), sib_par_at + delta - 1, sibling)
    for delta in range(1, 4):
        links.wait(par_half((zh + 4 - delta) % 4, 1 - core), sib_par_at + delta - 1)
    links.wait(par.at[zh], own_par_at)

    def row_at(t, block):
        return pl.ds(pl.multiple_of(t * TILES + block * 8, 8), 8)

    def state_rows(block):
        return pl.ds(pl.multiple_of(block * 128, 128), 128)

    def run_states(src, backward, es, block):
        decay = jnp.exp(-par[block, 0:MODES])

        def step(i, state):
            for r in range(8):
                t = i * 8 + r
                t = TOK - 1 - t if backward else t
                state = state * decay + src[row_at(t, block), :][None]
            return state

        state = lax.fori_loop(0, TOK // 8, step, jnp.zeros((MODES, 8, 128), F32))
        es[state_rows(block), :] = state.reshape(128, 128).astype(BF16)

    def send_states(sign, es, er, at, block, turn):
        for delta in range(1, 4):
            to = zh + sign * delta
            ok = to < 4 if sign > 0 else to >= 0
            links.send(es.at[state_rows(block), :], er.at[delta - 1, state_rows(block), :],
                       at + turn * 3 + delta - 1, (f, (to + 4) % 4), only=ok)

    def gather_states(sign, er, at, block, turn):
        carry[block] = jnp.zeros((MODES, 8, 128), F32)
        for delta in range(1, 4):
            source = zh - sign * delta

            @pl.when(source >= 0 if sign > 0 else source < 4)
            def _():
                links.wait(er.at[delta - 1, state_rows(block), :], at + turn * 3 + delta - 1)
                term = er[delta - 1, state_rows(block), :].astype(F32).reshape(MODES, 8, 128)
                if delta > 1:
                    term = term * jnp.exp(par[block, 0:MODES] * (-float(TOK) * (delta - 1)))
                carry[block] += term

    s_at = links.slot(12)
    for block in range(4):
        run_states(xs, False, es, block)
        send_states(1, es, er, s_at, block, block)

    wait_z(1)
    pass_z(1)
    send_y(-1)
    send_y(1)
    pass_y(0)

    left, right, far = ((x + 3) % 4) * 2 + core, ((x + 1) % 4) * 2 + core, ((x + 2) % 4) * 2 + core
    far_at = links.slot(2)

    def share(slot, h, at):
        ref = rows_of(cotb.at[slot], h)
        links.send(ref, ref, sib_at + at, sibling)

    links.wait(rows_of(cotb.at[left], 0), x_at)
    links.send(rows_of(cotb.at[left], 0), rows_of(cotb.at[left], 0), far_at, along_x(1))
    links.wait(rows_of(cotb.at[right], 1), x_at + 3)
    links.send(rows_of(cotb.at[right], 1), rows_of(cotb.at[right], 1), far_at + 1, along_x(-1))
    share(left, 0, 1)
    share(right, 1, 2)

    wait_z(2)
    pass_z(2)
    send_y(-2)
    send_y(2)
    pass_y(-1)
    pass_y(1)

    def tree(v):
        while v.shape[0] > 1:
            n = v.shape[0] // 2
            v = v[:n] + v[n:]
        return v[0]

    def convolve(block):
        decay = jnp.exp(-par[block, 0:MODES])
        weight = par[block, MODES:2 * MODES]

        def step(i, state):
            for r in range(8):
                rows = row_at(i * 8 + r, block)
                state = state * decay + xs[rows, :][None]
                cs[rows, :] = tree(state * weight)
            return state

        yend[block] = lax.fori_loop(0, TOK // 8, step, carry[block])

    def gate(t0, tile, k, rows, lanes):
        gated = qb[rows, lanes].astype(F32) * get(cs, t0, tile)
        gat_send[tile // 4, rows, pl.ds((k % 4) * 128, 128)] = gated.astype(BF16)

    links.wait(qb, load_at + 2)
    for block in range(4):
        gather_states(1, er, s_at, block, block)
        convolve(block)
        each_tile(gate, block)

    wait_z(3)
    pass_z(3)
    send_y(-3)
    send_y(3)
    pass_y(-2)
    pass_y(2)

    wait_z(4)
    send_y(4)
    pass_y(-3)
    pass_y(3)
    links.wait(rows_of(cotb.at[left], 1), x_at + 1)
    share(left, 1, 3)
    links.wait(rows_of(cotb.at[right], 0), x_at + 2)
    share(right, 0, 4)
    pass_y(4)
    for h in range(2):
        links.wait(rows_of(cotb.at[far], h), far_at + h)
        share(far, h, 5 + h)
    gat_at = links.slot(8)
    links.local(gat_send.at[b], gat.at[b], gat_at)
    for delta in range(1, 8):
        links.send(gat_send.at[(b + delta) % 8], gat.at[b], gat_at + delta, group(delta))
    for dz in range(8):
        wait_y(dz)

    other = 1 - 2 * core
    g_at = links.slot(8)

    def project(chip):
        total = jnp.zeros((2 * TOK, COLS), F32)
        for part in range(4):
            lhs = cotb[pl.ds(chip * 2, 2), :, pl.ds(part * 1024, 1024)].reshape(2 * TOK, 1024)
            total += jnp.dot(lhs, wbuf[pl.ds(part * 1024, 1024), :], preferred_element_type=F32)
        gsend[pl.ds(chip * 2, 2)] = total.astype(BF16).reshape(2, TOK, COLS)

    def return_chip(dx):
        chip = (x + dx) % 4
        for dc in range(2):
            to = chip * 2 + (core + dc) % 2
            if dx == 0 and dc == 0:
                links.local(gsend.at[b], grecv.at[b], g_at + b)
            else:
                links.send(gsend.at[to], grecv.at[b], g_at + b, (g * 8 + to, zh))

    links.wait(own, cot_at)
    links.wait(cotb.at[b + other], sib_at)
    project(x)
    return_chip(0)
    links.wait(rows_of(cotb.at[left + other], 0), sib_at + 1)
    links.wait(rows_of(cotb.at[left + other], 1), sib_at + 3)
    project((x + 3) % 4)
    return_chip(3)
    links.wait(rows_of(cotb.at[right + other], 1), sib_at + 2)
    links.wait(rows_of(cotb.at[right + other], 0), sib_at + 4)
    project((x + 1) % 4)
    return_chip(1)
    for h in range(2):
        links.wait(rows_of(cotb.at[far + other], h), sib_at + 5 + h)
    project((x + 2) % 4)
    return_chip(2)

    for delta in range(8):
        links.wait(gat.at[(b + 8 - delta) % 8], gat_at + delta)

    slabs = (4, 3, 5, 2, 6, 1, 7, 0)
    gy_at = links.slot(8 * 6)

    def slab_start(s, dy):
        zz = (z + slabs[s]) % 8
        return pl.multiple_of(((y + dy + 4) % 4) * 1024 + (zz % 2) * 512 + (zz // 2) * 128, 128)

    def slab_half(s, dy, h):
        return pl.ds(pl.multiple_of(slab_start(s, dy) + h * 64, 64), 64)

    def weight_slab(s):
        order = (2, 1, -1, 0)
        lhs = jnp.concatenate([cotb[:, :, pl.ds(slab_start(s, dy), 128)] for dy in order], axis=2)
        out = lax.dot_general(lhs.reshape(8 * TOK, 512), gat[...].reshape(8 * TOK, COLS),
                              (((0,), (0,)), ((), ())), preferred_element_type=F32)
        for i, dy in enumerate(order[:3]):
            gwp[pl.ds(slab_start(s, dy), 128), :] = out[i * 128:(i + 1) * 128].astype(BF16)
        vsum[s] = out[384:512]
        base = gy_at + s * 6
        links.send(gwp.at[slab_half(s, 2, 0), :], ra.at[s], base, along_y(1))
        links.send(gwp.at[slab_half(s, 2, 1), :], rb.at[s], base + 1, along_y(-1))
        links.send(gwp.at[slab_half(s, 1, 1), :], half_of(from_lo, s, 1), base + 2, along_y(1))
        links.send(gwp.at[slab_half(s, -1, 0), :], half_of(from_hi, s, 0), base + 3, along_y(-1))

    def half_of(ref, s, h):
        return ref.at[s, pl.ds(h * 64, 64), :]

    def add_slab(s):
        base = gy_at + s * 6
        for dy, h, term, dst, at in ((1, 0, ra, from_lo, 0), (-1, 1, rb, from_hi, 1)):
            links.wait(term.at[s], base + at)
            rows = slab_half(s, dy, h)
            gwp[rows, :] = (gwp[rows, :].astype(F32) + term[s].astype(F32)).astype(BF16)
            links.send(gwp.at[rows, :], half_of(dst, s, h), base + 4 + at, along_y(dy))

    gz_at = links.slot(7)

    def send_slab(s):
        base = gy_at + s * 6
        links.wait(half_of(from_lo, s, 1), base + 2)
        links.wait(half_of(from_hi, s, 0), base + 3)
        links.wait(half_of(from_lo, s, 0), base + 4)
        links.wait(half_of(from_hi, s, 1), base + 5)
        delta = slabs[s]
        total = vsum[s] + from_lo[s].astype(F32) + from_hi[s].astype(F32)
        if delta:
            zsend[delta - 1] = total.astype(BF16)
            links.send(zsend.at[delta - 1], zrecv.at[delta - 1], gz_at + delta - 1, along_z(delta))
        else:
            fin[...] = total

    for s in range(4):
        weight_slab(s)

    def grad_gate(t0, tile, k, rows, lanes):
        grad = grecv[tile // 4, rows, pl.ds((k % 4) * 128, 128)].astype(F32)
        gq[rows, lanes] = (grad * get(cs, t0, tile)).astype(BF16)
        put(gs, t0, tile, (grad * qb[rows, lanes].astype(F32)).astype(BF16).astype(F32))

    blocks = [(x + dx) % 4 for dx in (0, 1, 3, 2)]
    t_at = links.slot(12)
    for turn, block in enumerate(blocks):
        for c in range(2):
            links.wait(grecv.at[block * 2 + c], g_at + block * 2 + c)
        each_tile(grad_gate, block)
        run_states(gs, True, es2, block)
        send_states(-1, es2, er2, t_at, block, turn)
        add_slab(turn)
        weight_slab(4 + turn)
    out_at = links.slot(3)
    links.local(gq, gq_hbm, out_at)

    send_slab(0)
    send_slab(1)
    part = 4

    def adjoint(block):
        for m in range(0, MODES, part):
            rate = par[block, m:m + part]
            decay, growth = jnp.exp(-rate), jnp.exp(rate)
            weight = par[block, MODES + m:MODES + m + part]

            def step(i, carried):
                p, s, da, db = carried
                for r in range(8):
                    rows = row_at(TOK - 1 - (i * 8 + r), block)
                    xt = xs[rows, :][None]
                    p = p * decay + gs[rows, :][None]
                    da = da + p * xt
                    s = (s - xt) * growth
                    db = db + p * s
                    out = tree(p * weight)
                    if m:
                        out = out + cs[rows, :]
                    cs[rows, :] = out
                return p, s, da, db

            zero = jnp.zeros((part, 8, 128), F32)
            start = (carry[block, m:m + part], yend[block, m:m + part], zero, zero)
            _, _, da, db = lax.fori_loop(0, TOK // 8, step, start)
            ab[block, m:m + part] = da
            ab[block, MODES + m:MODES + m + part] = db * decay

    tp_at = links.slot(28)
    for turn, block in enumerate(blocks):
        gather_states(-1, er2, t_at, block, turn)
        adjoint(block)
        for delta in range(1, 8):
            to = pl.ds(((b + delta) % 8) * 4, 4)
            links.send(ab.at[block, to], tp_recv.at[delta - 1, block], tp_at + (delta - 1) * 4 + block,
                       group(delta))
        add_slab(4 + turn)
        send_slab(2 + turn)

    def grads(t0, tile, k, rows, lanes):
        grad = get(cs, t0, tile).astype(BF16).astype(F32)
        gk[rows, lanes] = (grad * vb[rows, lanes].astype(F32)).astype(BF16)
        gv[rows, lanes] = (grad * kb[rows, lanes].astype(F32)).astype(BF16)

    each_block(lambda block: each_tile(grads, block))
    links.local(gk, gk_hbm, out_at + 1)
    links.local(gv, gv_hbm, out_at + 2)

    r1[...] = ab[:, pl.ds(b * 4, 4)]
    for delta in range(1, 8):
        for block in range(4):
            links.wait(tp_recv.at[delta - 1, block], tp_at + (delta - 1) * 4 + block)
        r1[...] += tp_recv[delta - 1]
    c_at = links.slot(3)
    for delta in range(1, 4):
        links.send(r1.at[(zh + delta) % 4], ctx_recv.at[delta - 1], c_at + delta - 1, (f, (zh + delta) % 4))

    send_slab(6)
    send_slab(7)

    for delta in range(1, 8):
        links.wait(zrecv.at[delta - 1], gz_at + delta - 1)
        fin[...] += zrecv[delta - 1].astype(F32)
    fin_at = links.slot(2)
    for h in range(2):
        here = jnp.logical_and(x == zh, core == h)
        src = fin.at[pl.ds(h * 64, 64), :]
        links.send(src, gwo.at[core], fin_at + core, crossed(h), only=jnp.logical_not(here))
        links.local(src, gwo.at[core], fin_at + core, only=here)

    r2[...] = r1[zh]
    for delta in range(1, 4):
        links.wait(ctx_recv.at[delta - 1], c_at + delta - 1)
        r2[...] += ctx_recv[delta - 1]
    o_at = links.slot(7)
    for delta in range(1, 8):
        links.send(r2, g_recv.at[delta - 1], o_at + delta - 1, outer(delta))

    for delta in range(1, 8):
        links.wait(g_recv.at[delta - 1], o_at + delta - 1)
    total = jnp.zeros((4, 8, 128), F32)
    for source in range(8):
        delta = (g + 8 - source) % 8
        theirs = g_recv[jnp.maximum(delta - 1, 0)]
        total = total + jnp.where(delta == 0, r2[...], theirs)
    r3[...] = total
    e_at = links.slot(8)
    for delta in range(1, 8):
        links.send(r3, tot.at[pl.ds(b * 4, 4)], e_at + delta, group(delta))
    links.local(r3, tot.at[pl.ds(b * 4, 4)], e_at)

    gwo_at = links.slot(2)
    for h in range(2):
        links.wait(gwo.at[h], fin_at + h)
        links.local(gwo.at[h], gw_hbm.at[:, pl.ds(h * COLS, COLS)], gwo_at + h)
    for delta in range(8):
        links.wait(tot.at[pl.ds(((b + 8 - delta) % 8) * 4, 4)], e_at + delta)
    ab_at = links.slot(1)
    links.local(tot, ab_hbm, ab_at)

    links.wait(gq, out_at)
    links.wait(gk, out_at + 1)
    links.wait(gv, out_at + 2)
    for h in range(2):
        links.wait(gwo.at[h], gwo_at + h)
    links.wait(tot, ab_at)
    links.finish()


def shards(q_feat, k_feat, v_feat, residue, rate, w_out, cotangent):
    params = jnp.concatenate([rate.T, residue.T], axis=0).reshape(2 * MODES, 8, 128)
    anyspace = pl.BlockSpec(memory_space=pl.ANY)
    flat = (TOK, WIDTH)
    act = jax.ShapeDtypeStruct(flat, BF16)
    v = pltpu.VMEM
    grad_q, grad_k, grad_v, grad_weight, sums = pl.pallas_call(
        kernel,
        out_shape=(act, act, act, jax.ShapeDtypeStruct((64, 1024), F32),
                   jax.ShapeDtypeStruct((2 * MODES, 8, 128), F32)),
        in_specs=[anyspace] * 6,
        out_specs=[anyspace] * 5,
        scratch_shapes=[
            v(flat, BF16), v(flat, BF16), v(flat, BF16),
            v((4, 2 * MODES, 8, 128), F32),
            v((8, TOK, WIDTH), BF16), v((WIDTH, COLS), BF16),
            v((WIDTH, 128), F32), v((WIDTH, 128), F32), v((WIDTH, 128), F32),
            v((512, 128), BF16), v((3, 512, 128), BF16),
            v((512, 128), BF16), v((3, 512, 128), BF16),
            v((4, MODES, 8, 128), F32), v((4, MODES, 8, 128), F32),
            v((8, TOK, COLS), BF16), v((8, TOK, COLS), BF16),
            v((8, TOK, COLS), BF16), v((8, TOK, COLS), BF16),
            v((WIDTH, COLS), BF16),
            v((8, 64, COLS), BF16), v((8, 64, COLS), BF16),
            v((8, 128, COLS), BF16), v((8, 128, COLS), BF16),
            v((8, 128, COLS), F32),
            v((7, 128, COLS), BF16), v((7, 128, COLS), BF16),
            v((128, COLS), F32), v((2, 64, COLS), F32),
            v((4, 2 * MODES, 8, 128), F32),
            v((7, 4, 4, 8, 128), F32), v((4, 4, 8, 128), F32),
            v((3, 4, 8, 128), F32), v((4, 8, 128), F32),
            v((7, 4, 8, 128), F32), v((4, 8, 128), F32),
            v((2 * MODES, 8, 128), F32),
            v(flat, BF16), v(flat, BF16), v(flat, BF16),
            pltpu.SemaphoreType.DMA((N_SEND,)),
            pltpu.SemaphoreType.DMA((N_RECV,)),
        ],
        compiler_params=pltpu.CompilerParams(
            collective_id=0, has_side_effects=True, vmem_limit_bytes=60 * 1024 * 1024),
    )(q_feat[0], k_feat[0], v_feat[0], params, w_out, cotangent[0])
    sums = sums.reshape(2, MODES, 1024)
    grad_residue = sums[0].T
    grad_rate = -residue * sums[1].T
    return grad_q[None], grad_k[None], grad_v[None], grad_weight, grad_residue, grad_rate


def solution(mesh):
    act, modes, proj = P("fsdp", "ctx", None), P("ctx", None), P("fsdp", "ctx")
    return jax.shard_map(
        shards,
        mesh=mesh,
        in_specs=(act, act, act, modes, modes, proj, act),
        out_specs=(act, act, act, proj, modes, modes),
        check_vma=False,
    )
```

```python
import jax
import jax.numpy as jnp
from jax import lax
from jax.experimental import pallas as pl
from jax.experimental.pallas import tpu as pltpu
from jax.sharding import PartitionSpec as P

MESH = pl.DeviceIdType.MESH
F32, BF16 = jnp.float32, jnp.bfloat16
TOK = 128
WIDTH = 4096
TILES = 32
MODES = 16
COLS = 512
N_SEND = 256
N_RECV = 256


class Links:
    def __init__(self, send_sems, recv_sems):
        self.send_sems, self.recv_sems = send_sems, recv_sems
        self.sent, self.n_send, self.n_recv = [], 0, 0

    def slot(self, count=1):
        first = self.n_recv
        self.n_recv += count
        assert self.n_recv <= N_RECV
        return first

    def send(self, src, dst, recv, to, only=None):
        sem = self.send_sems.at[self.n_send]
        self.n_send += 1
        assert self.n_send <= N_SEND
        copy = pltpu.make_async_remote_copy(
            src_ref=src, dst_ref=dst, send_sem=sem, recv_sem=self.recv_sems.at[recv],
            device_id=to, device_id_type=MESH)
        if only is None:
            copy.start()
        else:
            pl.when(only)(copy.start)
        self.sent.append((copy, only))

    def local(self, src, dst, recv, only=None):
        copy = pltpu.make_async_copy(src, dst, self.recv_sems.at[recv])
        if only is None:
            copy.start()
        else:
            pl.when(only)(copy.start)

    def wait(self, dst, recv):
        pltpu.make_async_copy(dst, dst, self.recv_sems.at[recv]).wait()

    def finish(self):
        for copy, only in self.sent:
            if only is None:
                copy.wait_send()
            else:
                pl.when(only)(copy.wait_send)


def kernel(q_hbm, k_hbm, v_hbm, rate_hbm, res_hbm, w_hbm, cot_hbm,
           gq_hbm, gk_hbm, gv_hbm, gw_hbm, gres_hbm, grate_hbm,
           qb, kb, vb, modes, gmodes, par, cotb, wbuf, xs, cs, gs, es, er, es2, er2, carry, yend,
           gat_send, gat, gsend, grecv, gwp, ra, rb, from_lo, from_hi, vsum,
           zsend, zrecv, fin, gwo, ab, tp_recv, r1, ctx_recv, r2, g_recv, r3, tot,
           gq, gk, gv, send_sems, recv_sems):
    f, zh = lax.axis_index("fsdp"), lax.axis_index("ctx")
    y, zl, x, core = f // 16, (f // 8) % 2, (f // 2) % 4, f % 2
    b, g = f % 8, f // 8
    z = zh * 2 + zl
    links = Links(send_sems, recv_sems)

    def group(delta):
        return (g * 8 + (b + delta) % 8, zh)

    def outer(delta):
        return (((g + delta) % 8) * 8 + b, zh)

    def along_z(delta):
        to = (z + delta) % 8
        return (y * 16 + (to % 2) * 8 + b, to // 2)

    def along_y(delta):
        return (((y + delta) % 4) * 16 + zl * 8 + b, zh)

    def along_x(delta):
        return (g * 8 + ((x + delta) % 4) * 2 + core, zh)

    sibling = (g * 8 + x * 2 + 1 - core, zh)

    def crossed(h):
        return (g * 8 + zh * 2 + h, x)

    barrier = pltpu.get_barrier_semaphore()
    peers = [group(delta) for delta in range(1, 8)] + [along_z(delta) for delta in range(1, 8)]
    for delta in range(1, 4):
        for level in range(2):
            peers.append((((y + delta) % 4) * 16 + level * 8 + b, zh))
    for to in peers:
        pl.semaphore_signal(barrier, inc=1, device_id=to, device_id_type=MESH)

    @pl.when(x != zh)
    def _():
        for h in range(2):
            pl.semaphore_signal(barrier, inc=1, device_id=crossed(h), device_id_type=MESH)

    load_at = links.slot(3)
    for i, (src, dst) in enumerate(((k_hbm, kb), (v_hbm, vb), (q_hbm, qb))):
        links.local(src, dst, load_at + i)
    own = cotb.at[b]
    cot_at = links.slot(1)
    links.local(cot_hbm, own, cot_at)
    own_par_at = links.slot(2)
    links.local(rate_hbm, modes.at[0], own_par_at)
    links.local(res_hbm, modes.at[1], own_par_at + 1)

    links.wait(kb, load_at)
    links.wait(vb, load_at + 1)

    def put(ref, t0, tile, value):
        for i in range(2):
            start = (t0 + 8 * i) * TILES + tile
            ref[pl.ds(start, 8, stride=TILES), :] = value[8 * i:8 * i + 8]

    def get(ref, t0, tile):
        parts = [ref[pl.ds((t0 + 8 * i) * TILES + tile, 8, stride=TILES), :] for i in range(2)]
        return jnp.concatenate(parts, axis=0)

    def each_tile(body, block):
        def step(i, _):
            t0 = pl.multiple_of(i * 16, 16)
            for k in range(8):
                lanes = pl.ds(pl.multiple_of(block * 1024 + k * 128, 128), 128)
                body(t0, block * 8 + k, k, pl.ds(t0, 16), lanes)
            return 0
        lax.fori_loop(0, TOK // 16, step, 0)

    def each_block(body):
        def step(block, _):
            body(block)
            return 0
        lax.fori_loop(0, 4, step, 0)

    def mix(t0, tile, k, rows, lanes):
        product = kb[rows, lanes].astype(F32) * vb[rows, lanes].astype(F32)
        put(xs, t0, tile, product.astype(BF16).astype(F32))

    each_block(lambda block: each_tile(mix, block))

    for i in range(2):
        links.wait(modes.at[i], own_par_at + i)
        for s in range(8):
            par[zh, i * MODES:(i + 1) * MODES, s, :] = modes[i, :, s * 128:(s + 1) * 128]

    @pl.when(x != zh)
    def _():
        pl.semaphore_wait(barrier, len(peers) + 2)

    @pl.when(x == zh)
    def _():
        pl.semaphore_wait(barrier, len(peers))

    par_at = links.slot(3)
    sib_par_at = links.slot(3)

    def par_half(j, c):
        return par.at[j, pl.ds(c * MODES, MODES)]

    w_at = links.slot(2)
    w_rows = pl.ds(pl.multiple_of(f * 64, 64), 64)
    for h in range(2):
        here = jnp.logical_and(x == zh, core == h)
        src = w_hbm.at[:, pl.ds(h * COLS, COLS)]
        links.send(src, wbuf.at[w_rows, :], w_at + core, crossed(h), only=jnp.logical_not(here))
        links.local(src, wbuf.at[w_rows, :], w_at + core, only=here)
    for delta in range(1, 4):
        links.send(par_half(zh, core), par_half(zh, core), par_at + delta - 1,
                   (f, (zh + delta) % 4))

    half = TOK // 2
    x_at = links.slot(4)

    def rows_of(ref, h):
        return ref.at[pl.ds(h * half, half), :]

    def send_x(to, h, at):
        links.send(rows_of(cot_hbm, h), rows_of(own, h), x_at + at, along_x(to))

    send_x(1, 0, 0)
    send_x(-1, 1, 3)
    sib_at = links.slot(7)

    links.wait(wbuf.at[pl.ds(0, 64), :], w_at)
    links.wait(wbuf.at[pl.ds(0, 64), :], w_at + 1)

    def w_block(dy, dz, h=None):
        zz = (z + dz + 8) % 8
        start = ((y + dy + 4) % 4) * 1024 + (zz % 2) * 512 + (zz // 2) * 128
        if h is None:
            return wbuf.at[pl.ds(pl.multiple_of(start, 128), 128), :]
        return wbuf.at[pl.ds(pl.multiple_of(start + h * 64, 64), 64), :]

    up_at = links.slot(5)
    down_at = links.slot(5)
    wy_at = links.slot(8 * 6)

    def pass_z(step):
        for to, at in ((1, up_at), (-1, down_at)):
            ref = w_block(0, -to * step, None if step < 3 else (1 - to) // 2)
            links.send(ref, ref, at + step, along_z(to))

    def wait_z(step):
        for to, at in ((1, up_at), (-1, down_at)):
            links.wait(w_block(0, -to * step, None if step < 4 else (1 - to) // 2), at + step - 1)

    def send_y(dz):
        base = wy_at + (dz + 8) % 8 * 6
        for to, h, at in ((1, 0, 0), (-1, 1, 1), (1, 1, 2), (-1, 0, 3)):
            links.send(w_block(0, dz, h), w_block(0, dz, h), base + at, along_y(to))

    def pass_y(dz):
        base = wy_at + (dz + 8) % 8 * 6
        links.wait(w_block(-1, dz, 0), base)
        links.send(w_block(-1, dz, 0), w_block(-1, dz, 0), base + 4, along_y(1))
        links.wait(w_block(1, dz, 1), base + 1)
        links.send(w_block(1, dz, 1), w_block(1, dz, 1), base + 5, along_y(-1))

    def wait_y(dz):
        base = wy_at + (dz + 8) % 8 * 6
        links.wait(w_block(-1, dz, 1), base + 2)
        links.wait(w_block(1, dz, 0), base + 3)
        links.wait(w_block(2, dz, 0), base + 4)
        links.wait(w_block(2, dz, 1), base + 5)

    pass_z(0)
    send_y(0)
    send_x(1, 1, 1)
    send_x(-1, 0, 2)
    links.send(cot_hbm, own, sib_at, sibling)

    for delta in range(1, 4):
        source = (zh + 4 - delta) % 4
        links.wait(par_half(source, core), par_at + delta - 1)
        links.send(par_half(source, core), par_half(source, core), sib_par_at + delta - 1, sibling)
    for delta in range(1, 4):
        links.wait(par_half((zh + 4 - delta) % 4, 1 - core), sib_par_at + delta - 1)

    def row_at(t, block):
        return pl.ds(pl.multiple_of(t * TILES + block * 8, 8), 8)

    def state_rows(block):
        return pl.ds(pl.multiple_of(block * 128, 128), 128)

    def run_states(src, backward, es, block):
        decay = jnp.exp(-par[block, 0:MODES])

        def step(i, state):
            for r in range(8):
                t = i * 8 + r
                t = TOK - 1 - t if backward else t
                state = state * decay + src[row_at(t, block), :][None]
            return state

        state = lax.fori_loop(0, TOK // 8, step, jnp.zeros((MODES, 8, 128), F32))
        es[state_rows(block), :] = state.reshape(128, 128).astype(BF16)

    def send_states(sign, es, er, at, block, turn):
        for delta in range(1, 4):
            to = zh + sign * delta
            ok = to < 4 if sign > 0 else to >= 0
            links.send(es.at[state_rows(block), :], er.at[delta - 1, state_rows(block), :],
                       at + turn * 3 + delta - 1, (f, (to + 4) % 4), only=ok)

    def gather_states(sign, er, at, block, turn):
        carry[block] = jnp.zeros((MODES, 8, 128), F32)
        for delta in range(1, 4):
            source = zh - sign * delta

            @pl.when(source >= 0 if sign > 0 else source < 4)
            def _():
                links.wait(er.at[delta - 1, state_rows(block), :], at + turn * 3 + delta - 1)
                term = er[delta - 1, state_rows(block), :].astype(F32).reshape(MODES, 8, 128)
                if delta > 1:
                    term = term * jnp.exp(par[block, 0:MODES] * (-float(TOK) * (delta - 1)))
                carry[block] += term

    s_at = links.slot(12)
    for block in range(4):
        run_states(xs, False, es, block)
        send_states(1, es, er, s_at, block, block)

    wait_z(1)
    pass_z(1)
    send_y(-1)
    send_y(1)
    pass_y(0)

    left, right, far = ((x + 3) % 4) * 2 + core, ((x + 1) % 4) * 2 + core, ((x + 2) % 4) * 2 + core
    far_at = links.slot(2)

    def share(slot, h, at):
        ref = rows_of(cotb.at[slot], h)
        links.send(ref, ref, sib_at + at, sibling)

    links.wait(rows_of(cotb.at[left], 0), x_at)
    links.send(rows_of(cotb.at[left], 0), rows_of(cotb.at[left], 0), far_at, along_x(1))
    links.wait(rows_of(cotb.at[right], 1), x_at + 3)
    links.send(rows_of(cotb.at[right], 1), rows_of(cotb.at[right], 1), far_at + 1, along_x(-1))
    share(left, 0, 1)
    share(right, 1, 2)

    wait_z(2)
    pass_z(2)
    send_y(-2)
    send_y(2)
    pass_y(-1)
    pass_y(1)

    def tree(v):
        while v.shape[0] > 1:
            n = v.shape[0] // 2
            v = v[:n] + v[n:]
        return v[0]

    def convolve(block):
        decay = jnp.exp(-par[block, 0:MODES])
        weight = par[block, MODES:2 * MODES]

        def step(i, state):
            for r in range(8):
                rows = row_at(i * 8 + r, block)
                state = state * decay + xs[rows, :][None]
                cs[rows, :] = tree(state * weight)
            return state

        yend[block] = lax.fori_loop(0, TOK // 8, step, carry[block])

    def gate(t0, tile, k, rows, lanes):
        gated = qb[rows, lanes].astype(F32) * get(cs, t0, tile)
        gat_send[tile // 4, rows, pl.ds((k % 4) * 128, 128)] = gated.astype(BF16)

    links.wait(qb, load_at + 2)
    for block in range(4):
        gather_states(1, er, s_at, block, block)
        convolve(block)
        each_tile(gate, block)

    wait_z(3)
    pass_z(3)
    send_y(-3)
    send_y(3)
    pass_y(-2)
    pass_y(2)

    gat_at = links.slot(8)
    links.local(gat_send.at[b], gat.at[b], gat_at)
    for delta in range(1, 8):
        links.send(gat_send.at[(b + delta) % 8], gat.at[b], gat_at + delta, group(delta))
    wait_z(4)
    send_y(4)
    pass_y(-3)
    pass_y(3)
    links.wait(rows_of(cotb.at[left], 1), x_at + 1)
    share(left, 1, 3)
    links.wait(rows_of(cotb.at[right], 0), x_at + 2)
    share(right, 0, 4)
    pass_y(4)
    for h in range(2):
        links.wait(rows_of(cotb.at[far], h), far_at + h)
        share(far, h, 5 + h)
    for dz in range(8):
        wait_y(dz)

    other = 1 - 2 * core
    g_at = links.slot(8)

    def project(chip):
        total = jnp.zeros((2 * TOK, COLS), F32)
        for part in range(4):
            lhs = cotb[pl.ds(chip * 2, 2), :, pl.ds(part * 1024, 1024)].reshape(2 * TOK, 1024)
            total += jnp.dot(lhs, wbuf[pl.ds(part * 1024, 1024), :], preferred_element_type=F32)
        gsend[pl.ds(chip * 2, 2)] = total.astype(BF16).reshape(2, TOK, COLS)

    def return_chip(dx):
        chip = (x + dx) % 4
        for dc in range(2):
            to = chip * 2 + (core + dc) % 2
            if dx == 0 and dc == 0:
                links.local(gsend.at[b], grecv.at[b], g_at + b)
            else:
                links.send(gsend.at[to], grecv.at[b], g_at + b, (g * 8 + to, zh))

    links.wait(own, cot_at)
    links.wait(cotb.at[b + other], sib_at)
    project(x)
    return_chip(0)
    links.wait(rows_of(cotb.at[left + other], 0), sib_at + 1)
    links.wait(rows_of(cotb.at[left + other], 1), sib_at + 3)
    project((x + 3) % 4)
    return_chip(3)
    links.wait(rows_of(cotb.at[right + other], 1), sib_at + 2)
    links.wait(rows_of(cotb.at[right + other], 0), sib_at + 4)
    project((x + 1) % 4)
    return_chip(1)
    for h in range(2):
        links.wait(rows_of(cotb.at[far + other], h), sib_at + 5 + h)
    project((x + 2) % 4)
    return_chip(2)

    for delta in range(8):
        links.wait(gat.at[(b + 8 - delta) % 8], gat_at + delta)

    slabs = (4, 3, 5, 2, 6, 1, 7, 0)
    gy_at = links.slot(8 * 6)

    def slab_start(s, dy):
        zz = (z + slabs[s]) % 8
        return pl.multiple_of(((y + dy + 4) % 4) * 1024 + (zz % 2) * 512 + (zz // 2) * 128, 128)

    def slab_half(s, dy, h):
        return pl.ds(pl.multiple_of(slab_start(s, dy) + h * 64, 64), 64)

    def weight_slab(s):
        order = (2, 1, -1, 0)
        lhs = jnp.concatenate([cotb[:, :, pl.ds(slab_start(s, dy), 128)] for dy in order], axis=2)
        out = lax.dot_general(lhs.reshape(8 * TOK, 512), gat[...].reshape(8 * TOK, COLS),
                              (((0,), (0,)), ((), ())), preferred_element_type=F32)
        for i, dy in enumerate(order[:3]):
            gwp[pl.ds(slab_start(s, dy), 128), :] = out[i * 128:(i + 1) * 128].astype(BF16)
        vsum[s] = out[384:512]
        base = gy_at + s * 6
        links.send(gwp.at[slab_half(s, 2, 0), :], ra.at[s], base, along_y(1))
        links.send(gwp.at[slab_half(s, 2, 1), :], rb.at[s], base + 1, along_y(-1))
        links.send(gwp.at[slab_half(s, 1, 1), :], half_of(from_lo, s, 1), base + 2, along_y(1))
        links.send(gwp.at[slab_half(s, -1, 0), :], half_of(from_hi, s, 0), base + 3, along_y(-1))

    def half_of(ref, s, h):
        return ref.at[s, pl.ds(h * 64, 64), :]

    def add_slab(s):
        base = gy_at + s * 6
        for dy, h, term, dst, at in ((1, 0, ra, from_lo, 0), (-1, 1, rb, from_hi, 1)):
            links.wait(term.at[s], base + at)
            rows = slab_half(s, dy, h)
            gwp[rows, :] = (gwp[rows, :].astype(F32) + term[s].astype(F32)).astype(BF16)
            links.send(gwp.at[rows, :], half_of(dst, s, h), base + 4 + at, along_y(dy))

    gz_at = links.slot(7)

    def send_slab(s):
        base = gy_at + s * 6
        links.wait(half_of(from_lo, s, 1), base + 2)
        links.wait(half_of(from_hi, s, 0), base + 3)
        links.wait(half_of(from_lo, s, 0), base + 4)
        links.wait(half_of(from_hi, s, 1), base + 5)
        delta = slabs[s]
        total = vsum[s] + from_lo[s].astype(F32) + from_hi[s].astype(F32)
        if delta:
            zsend[delta - 1] = total.astype(BF16)
            links.send(zsend.at[delta - 1], zrecv.at[delta - 1], gz_at + delta - 1, along_z(delta))
        else:
            fin[...] = total

    for s in range(4):
        weight_slab(s)

    def grad_gate(t0, tile, k, rows, lanes):
        grad = grecv[tile // 4, rows, pl.ds((k % 4) * 128, 128)].astype(F32)
        gq[rows, lanes] = (grad * get(cs, t0, tile)).astype(BF16)
        put(gs, t0, tile, (grad * qb[rows, lanes].astype(F32)).astype(BF16).astype(F32))

    blocks = [(x + dx) % 4 for dx in (0, 1, 3, 2)]
    t_at = links.slot(12)
    for turn, block in enumerate(blocks):
        for c in range(2):
            links.wait(grecv.at[block * 2 + c], g_at + block * 2 + c)
        each_tile(grad_gate, block)
        run_states(gs, True, es2, block)
        send_states(-1, es2, er2, t_at, block, turn)
        add_slab(turn)
        weight_slab(4 + turn)
    out_at = links.slot(3)
    links.local(gq, gq_hbm, out_at)

    send_slab(0)
    send_slab(1)
    part = 4

    def adjoint(block):
        for m in range(0, MODES, part):
            rate = par[block, m:m + part]
            decay, growth = jnp.exp(-rate), jnp.exp(rate)
            weight = par[block, MODES + m:MODES + m + part]

            def step(i, carried):
                p, s, da, db = carried
                for r in range(8):
                    rows = row_at(TOK - 1 - (i * 8 + r), block)
                    xt = xs[rows, :][None]
                    p = p * decay + gs[rows, :][None]
                    da = da + p * xt
                    s = (s - xt) * growth
                    db = db + p * s
                    out = tree(p * weight)
                    if m:
                        out = out + cs[rows, :]
                    cs[rows, :] = out
                return p, s, da, db

            zero = jnp.zeros((part, 8, 128), F32)
            start = (carry[block, m:m + part], yend[block, m:m + part], zero, zero)
            _, _, da, db = lax.fori_loop(0, TOK // 8, step, start)
            ab[block, m:m + part] = da
            ab[block, MODES + m:MODES + m + part] = db * decay

    tp_at = links.slot(28)
    for turn, block in enumerate(blocks):
        gather_states(-1, er2, t_at, block, turn)
        adjoint(block)
        for delta in range(1, 8):
            to = pl.ds(((b + delta) % 8) * 4, 4)
            links.send(ab.at[block, to], tp_recv.at[delta - 1, block], tp_at + (delta - 1) * 4 + block,
                       group(delta))
        add_slab(4 + turn)
        send_slab(2 + turn)

    def grads(t0, tile, k, rows, lanes):
        grad = get(cs, t0, tile).astype(BF16).astype(F32)
        gk[rows, lanes] = (grad * vb[rows, lanes].astype(F32)).astype(BF16)
        gv[rows, lanes] = (grad * kb[rows, lanes].astype(F32)).astype(BF16)

    each_block(lambda block: each_tile(grads, block))
    links.local(gk, gk_hbm, out_at + 1)
    links.local(gv, gv_hbm, out_at + 2)

    r1[...] = ab[:, pl.ds(b * 4, 4)]
    for delta in range(1, 8):
        for block in range(4):
            links.wait(tp_recv.at[delta - 1, block], tp_at + (delta - 1) * 4 + block)
        r1[...] += tp_recv[delta - 1]
    c_at = links.slot(3)
    for delta in range(1, 4):
        links.send(r1.at[(zh + delta) % 4], ctx_recv.at[delta - 1], c_at + delta - 1, (f, (zh + delta) % 4))

    send_slab(6)
    send_slab(7)

    for delta in range(1, 8):
        links.wait(zrecv.at[delta - 1], gz_at + delta - 1)
        fin[...] += zrecv[delta - 1].astype(F32)
    fin_at = links.slot(2)
    for h in range(2):
        here = jnp.logical_and(x == zh, core == h)
        src = fin.at[pl.ds(h * 64, 64), :]
        links.send(src, gwo.at[core], fin_at + core, crossed(h), only=jnp.logical_not(here))
        links.local(src, gwo.at[core], fin_at + core, only=here)

    r2[...] = r1[zh]
    for delta in range(1, 4):
        links.wait(ctx_recv.at[delta - 1], c_at + delta - 1)
        r2[...] += ctx_recv[delta - 1]
    o_at = links.slot(7)
    for delta in range(1, 8):
        links.send(r2, g_recv.at[delta - 1], o_at + delta - 1, outer(delta))

    for delta in range(1, 8):
        links.wait(g_recv.at[delta - 1], o_at + delta - 1)
    total = jnp.zeros((4, 8, 128), F32)
    for source in range(8):
        delta = (g + 8 - source) % 8
        theirs = g_recv[jnp.maximum(delta - 1, 0)]
        total = total + jnp.where(delta == 0, r2[...], theirs)
    r3[...] = total
    e_at = links.slot(8)
    for delta in range(1, 8):
        links.send(r3, tot.at[pl.ds(b * 4, 4)], e_at + delta, group(delta))
    links.local(r3, tot.at[pl.ds(b * 4, 4)], e_at)

    gwo_at = links.slot(2)
    for h in range(2):
        links.wait(gwo.at[h], fin_at + h)
        links.local(gwo.at[h], gw_hbm.at[:, pl.ds(h * COLS, COLS)], gwo_at + h)
    for delta in range(8):
        links.wait(tot.at[pl.ds(((b + 8 - delta) % 8) * 4, 4)], e_at + delta)
    for s in range(8):
        lanes = slice(s * 128, (s + 1) * 128)
        gmodes[0, :, lanes] = tot[0:MODES, s, :]
        gmodes[1, :, lanes] = -modes[1, :, lanes] * tot[MODES:2 * MODES, s, :]
    ab_at = links.slot(2)
    links.local(gmodes.at[0], gres_hbm, ab_at)
    links.local(gmodes.at[1], grate_hbm, ab_at + 1)

    links.wait(gq, out_at)
    links.wait(gk, out_at + 1)
    links.wait(gv, out_at + 2)
    for h in range(2):
        links.wait(gwo.at[h], gwo_at + h)
    for i in range(2):
        links.wait(gmodes.at[i], ab_at + i)
    links.finish()


def shards(q_feat, k_feat, v_feat, residue, rate, w_out, cotangent):
    anyspace = pl.BlockSpec(memory_space=pl.ANY)
    flat = (TOK, WIDTH)
    act = jax.ShapeDtypeStruct(flat, BF16)
    v = pltpu.VMEM
    modes = jax.ShapeDtypeStruct((MODES, 1024), F32)
    grad_q, grad_k, grad_v, grad_weight, grad_residue, grad_rate = pl.pallas_call(
        kernel,
        out_shape=(act, act, act, jax.ShapeDtypeStruct((64, 1024), F32), modes, modes),
        in_specs=[anyspace] * 7,
        out_specs=[anyspace] * 6,
        scratch_shapes=[
            v(flat, BF16), v(flat, BF16), v(flat, BF16),
            v((2, MODES, 1024), F32), v((2, MODES, 1024), F32),
            v((4, 2 * MODES, 8, 128), F32),
            v((8, TOK, WIDTH), BF16), v((WIDTH, COLS), BF16),
            v((WIDTH, 128), F32), v((WIDTH, 128), F32), v((WIDTH, 128), F32),
            v((512, 128), BF16), v((3, 512, 128), BF16),
            v((512, 128), BF16), v((3, 512, 128), BF16),
            v((4, MODES, 8, 128), F32), v((4, MODES, 8, 128), F32),
            v((8, TOK, COLS), BF16), v((8, TOK, COLS), BF16),
            v((8, TOK, COLS), BF16), v((8, TOK, COLS), BF16),
            v((WIDTH, COLS), BF16),
            v((8, 64, COLS), BF16), v((8, 64, COLS), BF16),
            v((8, 128, COLS), BF16), v((8, 128, COLS), BF16),
            v((8, 128, COLS), F32),
            v((7, 128, COLS), BF16), v((7, 128, COLS), BF16),
            v((128, COLS), F32), v((2, 64, COLS), F32),
            v((4, 2 * MODES, 8, 128), F32),
            v((7, 4, 4, 8, 128), F32), v((4, 4, 8, 128), F32),
            v((3, 4, 8, 128), F32), v((4, 8, 128), F32),
            v((7, 4, 8, 128), F32), v((4, 8, 128), F32),
            v((2 * MODES, 8, 128), F32),
            v(flat, BF16), v(flat, BF16), v(flat, BF16),
            pltpu.SemaphoreType.DMA((N_SEND,)),
            pltpu.SemaphoreType.DMA((N_RECV,)),
        ],
        compiler_params=pltpu.CompilerParams(
            collective_id=0, has_side_effects=True, vmem_limit_bytes=60 * 1024 * 1024),
    )(q_feat[0], k_feat[0], v_feat[0], rate.T, residue.T, w_out, cotangent[0])
    return grad_q[None], grad_k[None], grad_v[None], grad_weight, grad_residue.T, grad_rate.T


def solution(mesh):
    act, modes, proj = P("fsdp", "ctx", None), P("ctx", None), P("fsdp", "ctx")
    return jax.shard_map(
        shards,
        mesh=mesh,
        in_specs=(act, act, act, modes, modes, proj, act),
        out_specs=(act, act, act, proj, modes, modes),
        check_vma=False,
    )
```

```python
import jax
import jax.numpy as jnp
from jax import lax
from jax.experimental import pallas as pl
from jax.experimental.pallas import tpu as pltpu
from jax.sharding import PartitionSpec as P

MESH = pl.DeviceIdType.MESH
F32, BF16 = jnp.float32, jnp.bfloat16
TOK = 128
WIDTH = 4096
TILES = 32
MODES = 16
COLS = 512
N_SEND = 256
N_RECV = 256


class Links:
    def __init__(self, send_sems, recv_sems):
        self.send_sems, self.recv_sems = send_sems, recv_sems
        self.sent, self.n_send, self.n_recv = [], 0, 0

    def slot(self, count=1):
        first = self.n_recv
        self.n_recv += count
        assert self.n_recv <= N_RECV
        return first

    def send(self, src, dst, recv, to, only=None):
        sem = self.send_sems.at[self.n_send]
        self.n_send += 1
        assert self.n_send <= N_SEND
        copy = pltpu.make_async_remote_copy(
            src_ref=src, dst_ref=dst, send_sem=sem, recv_sem=self.recv_sems.at[recv],
            device_id=to, device_id_type=MESH)
        if only is None:
            copy.start()
        else:
            pl.when(only)(copy.start)
        self.sent.append((copy, only))

    def local(self, src, dst, recv, only=None):
        copy = pltpu.make_async_copy(src, dst, self.recv_sems.at[recv])
        if only is None:
            copy.start()
        else:
            pl.when(only)(copy.start)

    def wait(self, dst, recv):
        pltpu.make_async_copy(dst, dst, self.recv_sems.at[recv]).wait()

    def finish(self):
        for copy, only in self.sent:
            if only is None:
                copy.wait_send()
            else:
                pl.when(only)(copy.wait_send)


def kernel(q_hbm, k_hbm, v_hbm, rate_hbm, res_hbm, w_hbm, cot_hbm,
           gq_hbm, gk_hbm, gv_hbm, gw_hbm, gres_hbm, grate_hbm,
           qb, kb, vb, modes, gmodes, par, cotb, wbuf, xs, cs, gs, es, er, es2, er2, carry, yend,
           gat_send, gat, gsend, grecv, gwp, ra, rb, from_lo, from_hi, vsum,
           zsend, zrecv, fin, gwo, ab, tp_recv, r1, ctx_recv, r2, g_recv, r3, tot,
           gq, gk, gv, send_sems, recv_sems):
    f, zh = lax.axis_index("fsdp"), lax.axis_index("ctx")
    y, zl, x, core = f // 16, (f // 8) % 2, (f // 2) % 4, f % 2
    b, g = f % 8, f // 8
    z = zh * 2 + zl
    links = Links(send_sems, recv_sems)

    def group(delta):
        return (g * 8 + (b + delta) % 8, zh)

    def outer(delta):
        return (((g + delta) % 8) * 8 + b, zh)

    def along_z(delta):
        to = (z + delta) % 8
        return (y * 16 + (to % 2) * 8 + b, to // 2)

    def along_y(delta):
        return (((y + delta) % 4) * 16 + zl * 8 + b, zh)

    def along_x(delta):
        return (g * 8 + ((x + delta) % 4) * 2 + core, zh)

    sibling = (g * 8 + x * 2 + 1 - core, zh)

    def crossed(h):
        return (g * 8 + zh * 2 + h, x)

    barrier = pltpu.get_barrier_semaphore()
    peers = [group(delta) for delta in range(1, 8)] + [along_z(delta) for delta in range(1, 8)]
    for delta in range(1, 4):
        for level in range(2):
            peers.append((((y + delta) % 4) * 16 + level * 8 + b, zh))
    for to in peers:
        pl.semaphore_signal(barrier, inc=1, device_id=to, device_id_type=MESH)

    @pl.when(x != zh)
    def _():
        for h in range(2):
            pl.semaphore_signal(barrier, inc=1, device_id=crossed(h), device_id_type=MESH)

    load_at = links.slot(3)
    for i, (src, dst) in enumerate(((k_hbm, kb), (v_hbm, vb), (q_hbm, qb))):
        links.local(src, dst, load_at + i)
    own = cotb.at[b]
    cot_at = links.slot(1)
    links.local(cot_hbm, own, cot_at)
    own_par_at = links.slot(2)
    links.local(rate_hbm, modes.at[0], own_par_at)
    links.local(res_hbm, modes.at[1], own_par_at + 1)

    links.wait(kb, load_at)
    links.wait(vb, load_at + 1)

    def put(ref, t0, tile, value):
        for i in range(2):
            start = (t0 + 8 * i) * TILES + tile
            ref[pl.ds(start, 8, stride=TILES), :] = value[8 * i:8 * i + 8]

    def get(ref, t0, tile):
        parts = [ref[pl.ds((t0 + 8 * i) * TILES + tile, 8, stride=TILES), :] for i in range(2)]
        return jnp.concatenate(parts, axis=0)

    def each_tile(body, block):
        def step(i, _):
            t0 = pl.multiple_of(i * 16, 16)
            for k in range(8):
                lanes = pl.ds(pl.multiple_of(block * 1024 + k * 128, 128), 128)
                body(t0, block * 8 + k, k, pl.ds(t0, 16), lanes)
            return 0
        lax.fori_loop(0, TOK // 16, step, 0)

    def each_block(body):
        def step(block, _):
            body(block)
            return 0
        lax.fori_loop(0, 4, step, 0)

    def mix(t0, tile, k, rows, lanes):
        product = kb[rows, lanes].astype(F32) * vb[rows, lanes].astype(F32)
        put(xs, t0, tile, product.astype(BF16).astype(F32))

    each_block(lambda block: each_tile(mix, block))

    for i in range(2):
        links.wait(modes.at[i], own_par_at + i)
        for s in range(8):
            par[zh, i * MODES:(i + 1) * MODES, s, :] = modes[i, :, s * 128:(s + 1) * 128]

    @pl.when(x != zh)
    def _():
        pl.semaphore_wait(barrier, len(peers) + 2)

    @pl.when(x == zh)
    def _():
        pl.semaphore_wait(barrier, len(peers))

    par_at = links.slot(3)
    sib_par_at = links.slot(3)

    def par_half(j, c):
        return par.at[j, pl.ds(c * MODES, MODES)]

    w_at = links.slot(2)
    w_rows = pl.ds(pl.multiple_of(f * 64, 64), 64)
    for h in range(2):
        here = jnp.logical_and(x == zh, core == h)
        src = w_hbm.at[:, pl.ds(h * COLS, COLS)]
        links.send(src, wbuf.at[w_rows, :], w_at + core, crossed(h), only=jnp.logical_not(here))
        links.local(src, wbuf.at[w_rows, :], w_at + core, only=here)
    for delta in range(1, 4):
        links.send(par_half(zh, core), par_half(zh, core), par_at + delta - 1,
                   (f, (zh + delta) % 4))

    half = TOK // 2
    x_at = links.slot(4)

    def rows_of(ref, h):
        return ref.at[pl.ds(h * half, half), :]

    def send_x(to, h, at):
        links.send(rows_of(cot_hbm, h), rows_of(own, h), x_at + at, along_x(to))

    send_x(1, 0, 0)
    send_x(-1, 1, 3)
    sib_at = links.slot(7)

    links.wait(wbuf.at[pl.ds(0, 64), :], w_at)
    links.wait(wbuf.at[pl.ds(0, 64), :], w_at + 1)

    def w_block(dy, dz, h=None):
        zz = (z + dz + 8) % 8
        start = ((y + dy + 4) % 4) * 1024 + (zz % 2) * 512 + (zz // 2) * 128
        if h is None:
            return wbuf.at[pl.ds(pl.multiple_of(start, 128), 128), :]
        return wbuf.at[pl.ds(pl.multiple_of(start + h * 64, 64), 64), :]

    up_at = links.slot(5)
    down_at = links.slot(5)
    wy_at = links.slot(8 * 6)

    def pass_z(step):
        for to, at in ((1, up_at), (-1, down_at)):
            ref = w_block(0, -to * step, None if step < 3 else (1 - to) // 2)
            links.send(ref, ref, at + step, along_z(to))

    def wait_z(step):
        for to, at in ((1, up_at), (-1, down_at)):
            links.wait(w_block(0, -to * step, None if step < 4 else (1 - to) // 2), at + step - 1)

    def send_y(dz):
        base = wy_at + (dz + 8) % 8 * 6
        for to, h, at in ((1, 0, 0), (-1, 1, 1), (1, 1, 2), (-1, 0, 3)):
            links.send(w_block(0, dz, h), w_block(0, dz, h), base + at, along_y(to))

    def pass_y(dz):
        base = wy_at + (dz + 8) % 8 * 6
        links.wait(w_block(-1, dz, 0), base)
        links.send(w_block(-1, dz, 0), w_block(-1, dz, 0), base + 4, along_y(1))
        links.wait(w_block(1, dz, 1), base + 1)
        links.send(w_block(1, dz, 1), w_block(1, dz, 1), base + 5, along_y(-1))

    def wait_y(dz):
        base = wy_at + (dz + 8) % 8 * 6
        links.wait(w_block(-1, dz, 1), base + 2)
        links.wait(w_block(1, dz, 0), base + 3)
        links.wait(w_block(2, dz, 0), base + 4)
        links.wait(w_block(2, dz, 1), base + 5)

    pass_z(0)
    send_y(0)
    send_x(1, 1, 1)
    send_x(-1, 0, 2)
    links.send(cot_hbm, own, sib_at, sibling)

    for delta in range(1, 4):
        source = (zh + 4 - delta) % 4
        links.wait(par_half(source, core), par_at + delta - 1)
        links.send(par_half(source, core), par_half(source, core), sib_par_at + delta - 1, sibling)
    for delta in range(1, 4):
        links.wait(par_half((zh + 4 - delta) % 4, 1 - core), sib_par_at + delta - 1)

    def row_at(t, block):
        return pl.ds(pl.multiple_of(t * TILES + block * 8, 8), 8)

    def state_rows(block):
        return pl.ds(pl.multiple_of(block * 128, 128), 128)

    def run_states(src, backward, es, block):
        decay = jnp.exp(-par[block, 0:MODES])

        def step(i, state):
            for r in range(8):
                t = i * 8 + r
                t = TOK - 1 - t if backward else t
                state = state * decay + src[row_at(t, block), :][None]
            return state

        state = lax.fori_loop(0, TOK // 8, step, jnp.zeros((MODES, 8, 128), F32))
        es[state_rows(block), :] = state.reshape(128, 128).astype(BF16)

    def send_states(sign, es, er, at, block, turn):
        for delta in range(1, 4):
            to = zh + sign * delta
            ok = to < 4 if sign > 0 else to >= 0
            links.send(es.at[state_rows(block), :], er.at[delta - 1, state_rows(block), :],
                       at + turn * 3 + delta - 1, (f, (to + 4) % 4), only=ok)

    def gather_states(sign, er, at, block, turn):
        carry[block] = jnp.zeros((MODES, 8, 128), F32)
        for delta in range(1, 4):
            source = zh - sign * delta

            @pl.when(source >= 0 if sign > 0 else source < 4)
            def _():
                links.wait(er.at[delta - 1, state_rows(block), :], at + turn * 3 + delta - 1)
                term = er[delta - 1, state_rows(block), :].astype(F32).reshape(MODES, 8, 128)
                if delta > 1:
                    term = term * jnp.exp(par[block, 0:MODES] * (-float(TOK) * (delta - 1)))
                carry[block] += term

    s_at = links.slot(12)
    for block in range(4):
        run_states(xs, False, es, block)
        send_states(1, es, er, s_at, block, block)

    wait_z(1)
    pass_z(1)
    send_y(-1)
    send_y(1)
    pass_y(0)

    left, right, far = ((x + 3) % 4) * 2 + core, ((x + 1) % 4) * 2 + core, ((x + 2) % 4) * 2 + core
    far_at = links.slot(2)

    def share(slot, h, at):
        ref = rows_of(cotb.at[slot], h)
        links.send(ref, ref, sib_at + at, sibling)

    links.wait(rows_of(cotb.at[left], 0), x_at)
    links.send(rows_of(cotb.at[left], 0), rows_of(cotb.at[left], 0), far_at, along_x(1))
    links.wait(rows_of(cotb.at[right], 1), x_at + 3)
    links.send(rows_of(cotb.at[right], 1), rows_of(cotb.at[right], 1), far_at + 1, along_x(-1))
    share(left, 0, 1)
    share(right, 1, 2)

    wait_z(2)
    pass_z(2)
    send_y(-2)
    send_y(2)
    pass_y(-1)
    pass_y(1)

    def tree(v):
        while v.shape[0] > 1:
            n = v.shape[0] // 2
            v = v[:n] + v[n:]
        return v[0]

    def convolve(block):
        decay = jnp.exp(-par[block, 0:MODES])
        weight = par[block, MODES:2 * MODES]

        def step(i, state):
            for r in range(8):
                rows = row_at(i * 8 + r, block)
                state = state * decay + xs[rows, :][None]
                cs[rows, :] = tree(state * weight)
            return state

        yend[block] = lax.fori_loop(0, TOK // 8, step, carry[block])

    def gate(t0, tile, k, rows, lanes):
        gated = qb[rows, lanes].astype(F32) * get(cs, t0, tile)
        gat_send[tile // 4, rows, pl.ds((k % 4) * 128, 128)] = gated.astype(BF16)

    links.wait(qb, load_at + 2)
    for block in range(4):
        gather_states(1, er, s_at, block, block)
        convolve(block)
        each_tile(gate, block)

    wait_z(3)
    pass_z(3)
    send_y(-3)
    send_y(3)
    pass_y(-2)
    pass_y(2)

    gat_at = links.slot(8)
    links.local(gat_send.at[b], gat.at[b], gat_at)
    for delta in range(1, 8):
        links.send(gat_send.at[(b + delta) % 8], gat.at[b], gat_at + delta, group(delta))
    wait_z(4)
    send_y(4)
    pass_y(-3)
    pass_y(3)
    links.wait(rows_of(cotb.at[left], 1), x_at + 1)
    share(left, 1, 3)
    links.wait(rows_of(cotb.at[right], 0), x_at + 2)
    share(right, 0, 4)
    pass_y(4)
    for h in range(2):
        links.wait(rows_of(cotb.at[far], h), far_at + h)
        share(far, h, 5 + h)
    for dz in range(8):
        wait_y(dz)

    other = 1 - 2 * core
    g_at = links.slot(8)

    def project(chip):
        total = jnp.zeros((2 * TOK, COLS), F32)
        for part in range(4):
            lhs = cotb[pl.ds(chip * 2, 2), :, pl.ds(part * 1024, 1024)].reshape(2 * TOK, 1024)
            total += jnp.dot(lhs, wbuf[pl.ds(part * 1024, 1024), :], preferred_element_type=F32)
        gsend[pl.ds(chip * 2, 2)] = total.astype(BF16).reshape(2, TOK, COLS)

    def return_chip(dx):
        chip = (x + dx) % 4
        for dc in range(2):
            to = chip * 2 + (core + dc) % 2
            if dx == 0 and dc == 0:
                links.local(gsend.at[b], grecv.at[b], g_at + b)
            else:
                links.send(gsend.at[to], grecv.at[b], g_at + b, (g * 8 + to, zh))

    links.wait(own, cot_at)
    links.wait(cotb.at[b + other], sib_at)
    links.wait(rows_of(cotb.at[left + other], 0), sib_at + 1)
    links.wait(rows_of(cotb.at[left + other], 1), sib_at + 3)
    links.wait(rows_of(cotb.at[right + other], 1), sib_at + 2)
    links.wait(rows_of(cotb.at[right + other], 0), sib_at + 4)
    for h in range(2):
        links.wait(rows_of(cotb.at[far + other], h), sib_at + 5 + h)
    for dx in (2, 3, 1, 0):
        project((x + dx) % 4)
        return_chip(dx)

    for delta in range(8):
        links.wait(gat.at[(b + 8 - delta) % 8], gat_at + delta)

    slabs = (4, 3, 5, 2, 6, 1, 7, 0)
    gy_at = links.slot(8 * 6)

    def slab_start(s, dy):
        zz = (z + slabs[s]) % 8
        return pl.multiple_of(((y + dy + 4) % 4) * 1024 + (zz % 2) * 512 + (zz // 2) * 128, 128)

    def slab_half(s, dy, h):
        return pl.ds(pl.multiple_of(slab_start(s, dy) + h * 64, 64), 64)

    def weight_slab(s):
        order = (2, 1, -1, 0)
        lhs = jnp.concatenate([cotb[:, :, pl.ds(slab_start(s, dy), 128)] for dy in order], axis=2)
        out = lax.dot_general(lhs.reshape(8 * TOK, 512), gat[...].reshape(8 * TOK, COLS),
                              (((0,), (0,)), ((), ())), preferred_element_type=F32)
        for i, dy in enumerate(order[:3]):
            gwp[pl.ds(slab_start(s, dy), 128), :] = out[i * 128:(i + 1) * 128].astype(BF16)
        vsum[s] = out[384:512]
        base = gy_at + s * 6
        links.send(gwp.at[slab_half(s, 2, 0), :], ra.at[s], base, along_y(1))
        links.send(gwp.at[slab_half(s, 2, 1), :], rb.at[s], base + 1, along_y(-1))
        links.send(gwp.at[slab_half(s, 1, 1), :], half_of(from_lo, s, 1), base + 2, along_y(1))
        links.send(gwp.at[slab_half(s, -1, 0), :], half_of(from_hi, s, 0), base + 3, along_y(-1))

    def half_of(ref, s, h):
        return ref.at[s, pl.ds(h * 64, 64), :]

    def add_slab(s):
        base = gy_at + s * 6
        for dy, h, term, dst, at in ((1, 0, ra, from_lo, 0), (-1, 1, rb, from_hi, 1)):
            links.wait(term.at[s], base + at)
            rows = slab_half(s, dy, h)
            gwp[rows, :] = (gwp[rows, :].astype(F32) + term[s].astype(F32)).astype(BF16)
            links.send(gwp.at[rows, :], half_of(dst, s, h), base + 4 + at, along_y(dy))

    gz_at = links.slot(7)

    def send_slab(s):
        base = gy_at + s * 6
        links.wait(half_of(from_lo, s, 1), base + 2)
        links.wait(half_of(from_hi, s, 0), base + 3)
        links.wait(half_of(from_lo, s, 0), base + 4)
        links.wait(half_of(from_hi, s, 1), base + 5)
        delta = slabs[s]
        total = vsum[s] + from_lo[s].astype(F32) + from_hi[s].astype(F32)
        if delta:
            zsend[delta - 1] = total.astype(BF16)
            links.send(zsend.at[delta - 1], zrecv.at[delta - 1], gz_at + delta - 1, along_z(delta))
        else:
            fin[...] = total

    for s in range(4):
        weight_slab(s)

    def grad_gate(t0, tile, k, rows, lanes):
        grad = grecv[tile // 4, rows, pl.ds((k % 4) * 128, 128)].astype(F32)
        gq[rows, lanes] = (grad * get(cs, t0, tile)).astype(BF16)
        put(gs, t0, tile, (grad * qb[rows, lanes].astype(F32)).astype(BF16).astype(F32))

    blocks = [(x + dx) % 4 for dx in (2, 1, 3, 0)]
    t_at = links.slot(12)
    for turn, block in enumerate(blocks):
        for c in range(2):
            links.wait(grecv.at[block * 2 + c], g_at + block * 2 + c)
        each_tile(grad_gate, block)
        run_states(gs, True, es2, block)
        send_states(-1, es2, er2, t_at, block, turn)
        add_slab(turn)
        weight_slab(4 + turn)
    out_at = links.slot(3)
    links.local(gq, gq_hbm, out_at)

    send_slab(0)
    send_slab(1)
    part = 4

    def adjoint(block):
        for m in range(0, MODES, part):
            rate = par[block, m:m + part]
            decay, growth = jnp.exp(-rate), jnp.exp(rate)
            weight = par[block, MODES + m:MODES + m + part]

            def step(i, carried):
                p, s, da, db = carried
                for r in range(8):
                    rows = row_at(TOK - 1 - (i * 8 + r), block)
                    xt = xs[rows, :][None]
                    p = p * decay + gs[rows, :][None]
                    da = da + p * xt
                    s = (s - xt) * growth
                    db = db + p * s
                    out = tree(p * weight)
                    if m:
                        out = out + cs[rows, :]
                    cs[rows, :] = out
                return p, s, da, db

            zero = jnp.zeros((part, 8, 128), F32)
            start = (carry[block, m:m + part], yend[block, m:m + part], zero, zero)
            _, _, da, db = lax.fori_loop(0, TOK // 8, step, start)
            ab[block, m:m + part] = da
            ab[block, MODES + m:MODES + m + part] = db * decay

    tp_at = links.slot(28)
    for turn, block in enumerate(blocks):
        gather_states(-1, er2, t_at, block, turn)
        adjoint(block)
        for delta in range(1, 8):
            to = pl.ds(((b + delta) % 8) * 4, 4)
            links.send(ab.at[block, to], tp_recv.at[delta - 1, block], tp_at + (delta - 1) * 4 + block,
                       group(delta))
        add_slab(4 + turn)
        send_slab(2 + turn)

    def grads(t0, tile, k, rows, lanes):
        grad = get(cs, t0, tile).astype(BF16).astype(F32)
        gk[rows, lanes] = (grad * vb[rows, lanes].astype(F32)).astype(BF16)
        gv[rows, lanes] = (grad * kb[rows, lanes].astype(F32)).astype(BF16)

    each_block(lambda block: each_tile(grads, block))
    links.local(gk, gk_hbm, out_at + 1)
    links.local(gv, gv_hbm, out_at + 2)

    r1[...] = ab[:, pl.ds(b * 4, 4)]
    for delta in range(1, 8):
        for block in range(4):
            links.wait(tp_recv.at[delta - 1, block], tp_at + (delta - 1) * 4 + block)
        r1[...] += tp_recv[delta - 1]
    c_at = links.slot(3)
    for delta in range(1, 4):
        links.send(r1.at[(zh + delta) % 4], ctx_recv.at[delta - 1], c_at + delta - 1, (f, (zh + delta) % 4))

    send_slab(6)
    send_slab(7)

    for delta in range(1, 8):
        links.wait(zrecv.at[delta - 1], gz_at + delta - 1)
        fin[...] += zrecv[delta - 1].astype(F32)
    fin_at = links.slot(2)
    for h in range(2):
        here = jnp.logical_and(x == zh, core == h)
        src = fin.at[pl.ds(h * 64, 64), :]
        links.send(src, gwo.at[core], fin_at + core, crossed(h), only=jnp.logical_not(here))
        links.local(src, gwo.at[core], fin_at + core, only=here)

    r2[...] = r1[zh]
    for delta in range(1, 4):
        links.wait(ctx_recv.at[delta - 1], c_at + delta - 1)
        r2[...] += ctx_recv[delta - 1]
    o_at = links.slot(7)
    for delta in range(1, 8):
        links.send(r2, g_recv.at[delta - 1], o_at + delta - 1, outer(delta))

    for delta in range(1, 8):
        links.wait(g_recv.at[delta - 1], o_at + delta - 1)
    total = jnp.zeros((4, 8, 128), F32)
    for source in range(8):
        delta = (g + 8 - source) % 8
        theirs = g_recv[jnp.maximum(delta - 1, 0)]
        total = total + jnp.where(delta == 0, r2[...], theirs)
    r3[...] = total
    e_at = links.slot(8)
    for delta in range(1, 8):
        links.send(r3, tot.at[pl.ds(b * 4, 4)], e_at + delta, group(delta))
    links.local(r3, tot.at[pl.ds(b * 4, 4)], e_at)

    gwo_at = links.slot(2)
    for h in range(2):
        links.wait(gwo.at[h], fin_at + h)
        links.local(gwo.at[h], gw_hbm.at[:, pl.ds(h * COLS, COLS)], gwo_at + h)
    for delta in range(8):
        links.wait(tot.at[pl.ds(((b + 8 - delta) % 8) * 4, 4)], e_at + delta)
    for s in range(8):
        lanes = slice(s * 128, (s + 1) * 128)
        gmodes[0, :, lanes] = tot[0:MODES, s, :]
        gmodes[1, :, lanes] = -modes[1, :, lanes] * tot[MODES:2 * MODES, s, :]
    ab_at = links.slot(2)
    links.local(gmodes.at[0], gres_hbm, ab_at)
    links.local(gmodes.at[1], grate_hbm, ab_at + 1)

    links.wait(gq, out_at)
    links.wait(gk, out_at + 1)
    links.wait(gv, out_at + 2)
    for h in range(2):
        links.wait(gwo.at[h], gwo_at + h)
    for i in range(2):
        links.wait(gmodes.at[i], ab_at + i)
    links.finish()


def shards(q_feat, k_feat, v_feat, residue, rate, w_out, cotangent):
    anyspace = pl.BlockSpec(memory_space=pl.ANY)
    flat = (TOK, WIDTH)
    act = jax.ShapeDtypeStruct(flat, BF16)
    v = pltpu.VMEM
    modes = jax.ShapeDtypeStruct((MODES, 1024), F32)
    grad_q, grad_k, grad_v, grad_weight, grad_residue, grad_rate = pl.pallas_call(
        kernel,
        out_shape=(act, act, act, jax.ShapeDtypeStruct((64, 1024), F32), modes, modes),
        in_specs=[anyspace] * 7,
        out_specs=[anyspace] * 6,
        scratch_shapes=[
            v(flat, BF16), v(flat, BF16), v(flat, BF16),
            v((2, MODES, 1024), F32), v((2, MODES, 1024), F32),
            v((4, 2 * MODES, 8, 128), F32),
            v((8, TOK, WIDTH), BF16), v((WIDTH, COLS), BF16),
            v((WIDTH, 128), F32), v((WIDTH, 128), F32), v((WIDTH, 128), F32),
            v((512, 128), BF16), v((3, 512, 128), BF16),
            v((512, 128), BF16), v((3, 512, 128), BF16),
            v((4, MODES, 8, 128), F32), v((4, MODES, 8, 128), F32),
            v((8, TOK, COLS), BF16), v((8, TOK, COLS), BF16),
            v((8, TOK, COLS), BF16), v((8, TOK, COLS), BF16),
            v((WIDTH, COLS), BF16),
            v((8, 64, COLS), BF16), v((8, 64, COLS), BF16),
            v((8, 128, COLS), BF16), v((8, 128, COLS), BF16),
            v((8, 128, COLS), F32),
            v((7, 128, COLS), BF16), v((7, 128, COLS), BF16),
            v((128, COLS), F32), v((2, 64, COLS), F32),
            v((4, 2 * MODES, 8, 128), F32),
            v((7, 4, 4, 8, 128), F32), v((4, 4, 8, 128), F32),
            v((3, 4, 8, 128), F32), v((4, 8, 128), F32),
            v((7, 4, 8, 128), F32), v((4, 8, 128), F32),
            v((2 * MODES, 8, 128), F32),
            v(flat, BF16), v(flat, BF16), v(flat, BF16),
            pltpu.SemaphoreType.DMA((N_SEND,)),
            pltpu.SemaphoreType.DMA((N_RECV,)),
        ],
        compiler_params=pltpu.CompilerParams(
            collective_id=0, has_side_effects=True, vmem_limit_bytes=60 * 1024 * 1024),
    )(q_feat[0], k_feat[0], v_feat[0], rate.T, residue.T, w_out, cotangent[0])
    return grad_q[None], grad_k[None], grad_v[None], grad_weight, grad_residue.T, grad_rate.T


def solution(mesh):
    act, modes, proj = P("fsdp", "ctx", None), P("ctx", None), P("fsdp", "ctx")
    return jax.shard_map(
        shards,
        mesh=mesh,
        in_specs=(act, act, act, modes, modes, proj, act),
        out_specs=(act, act, act, proj, modes, modes),
        check_vma=False,
    )
```
